32 devices in a mesh: band: 8 (over z, x), grid: 4 (over y, core).
Axes of the slice: x: 2, y: 2, z: 4, core: 2. Of those that a mesh axis runs over, the one named last changes fastest.
Arguments:
- trial_bands: float32 [16, 40, 32, 128], P('band', 'grid'), may hold values from -6 to 6
- potential: float32 [40, 32, 128], P('grid'), may hold values from -2 to 0
Outputs:
- filtered: float32 [16, 40, 32, 128], P('band', 'grid')
- projected: float32 [16, 16], P('band')
- residual_norms: float32 [16], P('band')
The draws below stay inside these ranges and needn't reach their ends.
All inputs are finite; a program needn't handle non-finite values.
Results may differ from the reference program's by a relative error of at most 0.00016.
Values sent between devices are 32-bit elements; how exact they have to be, the bound alone decides.
A program may use at most 64 MiB of HBM per device.

```python
import jax
import jax.numpy as jnp
from jax import lax

NX = 32
NY = 128
BANDS = 16
NZ = 40


def level_of(stream_key, shape, pieces, smallest, largest):
    loudness, own = 1.0, jax.random.fold_in(stream_key, 6)
    for position, parts in pieces:
        steps = jnp.exp(jax.random.uniform(jax.random.fold_in(own, position), (parts,), jnp.float32, smallest / len(pieces), largest / len(pieces)))
        loudness = loudness * jnp.repeat(steps, shape[position] // parts).reshape([-1 if axis == position else 1 for axis in range(len(shape))])
    return loudness


def centred(own_key, shape, width, most, cuts=(), kind=jnp.bfloat16):
    values = width * jax.random.normal(own_key, shape, jnp.float32)
    if cuts:
        values = values * level_of(own_key, shape, cuts, -0.22, 0.18)
    return jnp.clip(values, -most, most).astype(kind)


def setup_inputs(seed: int = 0) -> dict:
    splits = jax.random.split(jax.random.key(seed), 3)
    return {
        "trial_bands": centred(splits[0], (BANDS, NZ, NX, NY), 1.0, 6.0, ((0, 8), (1, 4)), jnp.float32),
        "potential": jnp.clip(-2.0 + 2.0 * jax.random.uniform(splits[1], (NZ, NX, NY), jnp.float32) ** level_of(splits[1], (NZ, NX, NY), ((0, 4),), -0.2, 0.2), -2.0, 0.0),
    }


CENTER = 4.25
HALF_WIDTH = 3.75
LOWEST = -2.0
SIGMA_ONE = HALF_WIDTH / (LOWEST - CENTER)
FOUR_THIRDS = 4.0 / 3.0
TWELFTH = 1.0 / 12.0
filter_degree = 4

def hamiltonian(field_in, potential):
    near_sum = jnp.roll(field_in, 1, 1) + jnp.roll(field_in, -1, 1)
    near_sum = near_sum + jnp.roll(field_in, 1, 2) + jnp.roll(field_in, -1, 2)
    near_sum = near_sum + jnp.roll(field_in, 1, 3) + jnp.roll(field_in, -1, 3)
    far_sum = jnp.roll(field_in, 2, 1) + jnp.roll(field_in, -2, 1)
    far_sum = far_sum + jnp.roll(field_in, 2, 2) + jnp.roll(field_in, -2, 2)
    far_sum = far_sum + jnp.roll(field_in, 2, 3) + jnp.roll(field_in, -2, 3)
    kinetic = 0.5 * (7.5 * field_in - FOUR_THIRDS * near_sum + TWELFTH * far_sum)
    return kinetic + potential * field_in

def chebyshev(start_block, operate):
    sigma_now = SIGMA_ONE
    previous = start_block
    current = (operate(start_block) - CENTER * start_block) * (SIGMA_ONE / HALF_WIDTH)
    for repeat_index in range(filter_degree - 1):
        sigma_next = 1.0 / (2.0 / SIGMA_ONE - sigma_now)
        following = (operate(current) - CENTER * current) * (2.0 * sigma_next / HALF_WIDTH) - sigma_now * sigma_next * previous
        previous, current, sigma_now = (current, following, sigma_next)
    return current

def reference(trial_bands, potential):

    def operate(field_in):
        return hamiltonian(field_in, potential)
    filtered = chebyshev(trial_bands, operate)
    applied = operate(filtered)
    flat_bands = filtered.reshape(BANDS, -1)
    flat_image = applied.reshape(BANDS, -1)
    inverse_cells = 1.0 / (NZ * NX * NY)
    margin = jnp.dot(flat_bands.astype(jnp.float32), flat_bands.T.astype(jnp.float32), precision=lax.Precision.HIGHEST, preferred_element_type=jnp.float32) * inverse_cells
    subspace = jnp.dot(flat_image.astype(jnp.float32), flat_bands.T.astype(jnp.float32), precision=lax.Precision.HIGHEST, preferred_element_type=jnp.float32) * inverse_cells
    image_norms = jnp.sum(flat_image * flat_image, axis=1) * inverse_cells
    factor = jnp.linalg.cholesky(margin)
    coefficients = lax.linalg.triangular_solve(factor, subspace.T, left_side=True, lower=True)
    projected = lax.linalg.triangular_solve(factor, coefficients.T, left_side=True, lower=True)
    residual_norms = image_norms - jnp.sum(coefficients * coefficients, axis=0)
    return (filtered, projected, residual_norms)
```

```python
import functools

import jax
import jax.numpy as jnp
from jax import lax
from jax.experimental import pallas as pl
from jax.experimental.pallas import tpu as pltpu
from jax.sharding import PartitionSpec as P

CENTER = 4.25
HALF_WIDTH = 3.75
LOWEST = -2.0
SIGMA_ONE = HALF_WIDTH / (LOWEST - CENTER)
MESH = pl.DeviceIdType.MESH
HIGHEST = lax.Precision.HIGHEST
CONTRACT_LANES = (((1,), (1,)), ((), ()))


def filter_steps():
    sigma_now = SIGMA_ONE
    steps = [(SIGMA_ONE / HALF_WIDTH, 0.0)]
    for _ in range(3):
        sigma_next = 1.0 / (2.0 / SIGMA_ONE - sigma_now)
        steps.append((2.0 * sigma_next / HALF_WIDTH, sigma_now * sigma_next))
        sigma_now = sigma_next
    return steps


def kernel(
    sizes,
    x_hbm,
    v_hbm,
    f_out,
    projected_out,
    residual_out,
    x0,
    vp,
    y1,
    y2,
    y3,
    y4,
    image,
    f_share,
    f_all,
    h_all,
    part_a,
    part_b,
    halo_send,
    halo_recv,
    f_send,
    f_recv,
    h_send,
    h_recv,
    a_send,
    a_recv,
    b_send,
    b_recv,
    local_sem,
):
    nb, nz, nx, n_band, n_grid, share, width, cells = sizes
    rows = nz * nx
    bands = nb * n_band
    me = lax.axis_index("band")
    slab = lax.axis_index("grid")
    right = lax.rem(slab + 1, n_grid)
    left = lax.rem(slab + n_grid - 1, n_grid)
    ny = x0.shape[-1]

    own = [
        pltpu.make_async_copy(x_hbm, x0.at[:, pl.ds(4 * nx, rows)], local_sem.at[0]),
        pltpu.make_async_copy(v_hbm, vp.at[pl.ds(2 * nx, rows)], local_sem.at[1]),
    ]
    for copy in own:
        copy.start()

    barrier = pltpu.get_barrier_semaphore()

    def greet_band(d, carry):
        pl.semaphore_signal(
            barrier, inc=1, device_id=(lax.rem(me + d, n_band), slab), device_id_type=MESH
        )
        return carry

    def greet_grid(d, carry):
        pl.semaphore_signal(
            barrier, inc=1, device_id=(me, lax.rem(slab + d, n_grid)), device_id_type=MESH
        )
        return carry

    lax.fori_loop(1, n_grid, greet_grid, 0)
    lax.fori_loop(1, n_band, greet_band, 0)
    pl.semaphore_wait(barrier, n_band + n_grid - 2)

    def halo_copy(index, src, dst, to):
        return pltpu.make_async_remote_copy(
            src_ref=src,
            dst_ref=dst,
            send_sem=halo_send.at[index],
            recv_sem=halo_recv.at[index],
            device_id=(me, to),
            device_id_type=MESH,
        )

    def up(index, src, first, dst, depth):
        return halo_copy(
            index,
            src.at[:, pl.ds((first + nz - depth) * nx, depth * nx)],
            dst.at[:, pl.ds(0, depth * nx)],
            right,
        )

    def down(index, src, first, dst, depth):
        return halo_copy(
            index,
            src.at[:, pl.ds(first * nx, depth * nx)],
            dst.at[:, pl.ds((nz + depth) * nx, depth * nx)],
            left,
        )

    swap_x = [up(0, x_hbm, 0, x0, 4), down(1, x_hbm, 0, x0, 4)]
    swap_v = [
        halo_copy(2, v_hbm.at[pl.ds((nz - 2) * nx, 2 * nx)], vp.at[pl.ds(0, 2 * nx)], right),
        halo_copy(3, v_hbm.at[pl.ds(0, 2 * nx)], vp.at[pl.ds((nz + 2) * nx, 2 * nx)], left),
    ]
    swap_2 = [up(4, y2, 4, y2, 4), down(5, y2, 4, y2, 4)]
    swap_4 = [up(6, y4, 2, y4, 2), down(7, y4, 2, y4, 2)]
    for copy in swap_x + swap_v:
        copy.start()

    steps = filter_steps()

    def planes(lo, hi, src, src_halo, dsts, scale, center, prev=None, prev_halo=0, weight=0.0):
        def at(ref, band, halo, plane):
            return ref[band, pl.ds(pl.multiple_of((plane + halo) * nx, nx), nx), :]

        def body(pair, carry):
            first = lo + 2 * pair
            for plane in (first, first + 1):
                local = vp[pl.ds(pl.multiple_of((plane + 2) * nx, nx), nx), :]
                local = (local + (3.75 - center)) * scale
                for band in range(nb):
                    here = at(src, band, src_halo, plane)
                    near = at(src, band, src_halo, plane - 1) + at(src, band, src_halo, plane + 1)
                    far = at(src, band, src_halo, plane - 2) + at(src, band, src_halo, plane + 2)
                    near += pltpu.roll(here, 1, 0) + pltpu.roll(here, nx - 1, 0)
                    far += pltpu.roll(here, 2, 0) + pltpu.roll(here, nx - 2, 0)
                    near += pltpu.roll(here, 1, 1) + pltpu.roll(here, ny - 1, 1)
                    far += pltpu.roll(here, 2, 1) + pltpu.roll(here, ny - 2, 1)
                    value = local * here - near * (scale * 2.0 / 3.0) + far * (scale / 24.0)
                    if prev is not None:
                        value = value - weight * at(prev, band, prev_halo, plane)
                    for dst, halo in dsts:
                        dst[band, pl.ds(pl.multiple_of((plane + halo) * nx, nx), nx), :] = value
            return carry

        lax.fori_loop(0, (hi - lo) // 2, body, 0)

    for copy in own:
        copy.wait()

    step_1 = functools.partial(planes, src=x0, src_halo=4, dsts=[(y1, 2)], scale=steps[0][0], center=CENTER)
    step_1(2, nz - 2)
    for copy in swap_x + swap_v:
        copy.wait()
    step_1(-2, 2)
    step_1(nz - 2, nz + 2)

    step_2 = functools.partial(
        planes, src=y1, src_halo=2, dsts=[(y2, 4)], scale=steps[1][0], center=CENTER,
        prev=x0, prev_halo=4, weight=steps[1][1],
    )
    step_2(0, 4)
    swap_2[1].start()
    step_2(nz - 4, nz)
    swap_2[0].start()
    step_2(4, nz - 4)

    step_3 = functools.partial(
        planes, src=y2, src_halo=4, dsts=[(y3, 2)], scale=steps[2][0], center=CENTER,
        prev=y1, prev_halo=2, weight=steps[2][1],
    )
    step_3(2, nz - 2)
    for copy in swap_2:
        copy.wait()
    step_3(-2, 2)
    step_3(nz - 2, nz + 2)

    step_4 = functools.partial(
        planes, src=y3, src_halo=2, dsts=[(y4, 2), (f_share, 0)], scale=steps[3][0], center=CENTER,
        prev=y2, prev_halo=4, weight=steps[3][1],
    )
    step_4(0, 2)
    swap_4[1].start()
    step_4(nz - 2, nz)
    swap_4[0].start()
    step_4(2, nz - 2)

    padded = share * n_band
    if padded != rows:
        f_share[:, rows:, :] = jnp.zeros((nb, padded - rows, ny), jnp.float32)
        image[:, rows:, :] = jnp.zeros((nb, padded - rows, ny), jnp.float32)

    def to_band(src, dst, send, recv, d):
        partner = lax.rem(me + d, n_band)
        return pltpu.make_async_remote_copy(
            src_ref=src.at[:, pl.ds(pl.multiple_of(partner * share, 8), share)],
            dst_ref=dst.at[me],
            send_sem=send.at[d],
            recv_sem=recv.at[n_band - d],
            device_id=(partner, slab),
            device_id_type=MESH,
        )

    def start_band(src, dst, send, recv):
        def body(d, carry):
            to_band(src, dst, send, recv, d).start()
            return carry

        lax.fori_loop(1, n_band, body, 0)

    def wait_band(src, dst, send, recv):
        def body(d, carry):
            to_band(src, dst, send, recv, d).wait()
            return carry

        lax.fori_loop(1, n_band, body, 0)

    start_band(f_share, f_all, f_send, f_recv)
    out_copy = pltpu.make_async_copy(f_share.at[:, pl.ds(0, rows)], f_out, local_sem.at[2])
    out_copy.start()

    last = functools.partial(planes, src=y4, src_halo=2, dsts=[(image, 0)], scale=1.0, center=0.0)
    last(2, nz - 2)
    for copy in swap_4:
        copy.wait()
    last(0, 2)
    last(nz - 2, nz)
    start_band(image, h_all, h_send, h_recv)

    own_rows = pl.ds(pl.multiple_of(me * share, 8), share)
    f_all[me] = f_share[:, own_rows, :]
    h_all[me] = image[:, own_rows, :]

    def on_lanes(ref):
        whole = ref[...]
        tiles = [
            whole[:, :, 8 * t : 8 * t + 8, :].reshape(bands * 8, ny) for t in range(share // 8)
        ]
        return jnp.concatenate(tiles, axis=1)

    stretched = bands * 8
    same = (
        lax.broadcasted_iota(jnp.int32, (stretched, stretched), 0) % 8
        == lax.broadcasted_iota(jnp.int32, (stretched, stretched), 1) % 8
    )
    column = lax.broadcasted_iota(jnp.int32, (stretched, width), 0) // 8
    lane = lax.broadcasted_iota(jnp.int32, (stretched, width), 1)

    def folded(gram, offset):
        gram = jnp.where(same, gram, 0.0).reshape(bands, 8, stretched).sum(axis=1)
        pick = jnp.where(column + offset == lane, 1.0, 0.0)
        return jnp.dot(gram, pick, precision=HIGHEST, preferred_element_type=jnp.float32)

    wait_band(f_share, f_all, f_send, f_recv)
    filtered = on_lanes(f_all)
    margin = lax.dot_general(
        filtered, filtered, CONTRACT_LANES, precision=HIGHEST, preferred_element_type=jnp.float32
    )
    top = folded(margin, 0)
    wait_band(image, h_all, h_send, h_recv)
    images = on_lanes(h_all)
    mixed = lax.dot_general(
        filtered, images, CONTRACT_LANES, precision=HIGHEST, preferred_element_type=jnp.float32
    )
    top = top + folded(mixed, bands)
    whole = h_all[...]
    squares = (whole * whole).sum(axis=2).reshape(bands, ny)
    norms = lax.dot_general(
        jnp.ones((8, ny), jnp.float32),
        squares,
        CONTRACT_LANES,
        precision=HIGHEST,
        preferred_element_type=jnp.float32,
    )
    part_a[me, 0:bands, :] = top
    part_a[me, bands:, :] = jnp.zeros((8, width), jnp.float32)
    part_a[me, bands:, 0:bands] = norms

    def sum_over(part, count, here, target, send, recv):
        def copy(d):
            return pltpu.make_async_remote_copy(
                src_ref=part.at[here],
                dst_ref=part.at[here],
                send_sem=send.at[d],
                recv_sem=recv.at[count - d],
                device_id=target(lax.rem(here + d, count)),
                device_id_type=MESH,
            )

        def start(d, carry):
            copy(d).start()
            return carry

        def wait(d, carry):
            copy(d).wait()
            return carry

        lax.fori_loop(1, count, start, 0)
        lax.fori_loop(1, count, wait, 0)
        return jnp.sum(part[...], axis=0)

    part_b[slab] = sum_over(part_a, n_band, me, lambda j: (j, slab), a_send, a_recv)
    total = sum_over(part_b, n_grid, slab, lambda j: (me, j), b_send, b_recv) * (1.0 / cells)

    row_of = lax.broadcasted_iota(jnp.int32, (bands, width), 0)
    lane_of = lax.broadcasted_iota(jnp.int32, (bands, width), 1)
    work = total[0:bands]
    work = jnp.where(lane_of == row_of + 2 * bands, 1.0, work)
    for k in range(bands):
        pivot = work[k : k + 1, k : k + 1]
        inverse = lax.rsqrt(pivot)
        inverse = inverse * (1.5 - 0.5 * pivot * inverse * inverse)
        row = work[k : k + 1, :] * inverse
        factor_column = work[:, k : k + 1] * inverse
        below = work - factor_column * row
        work = jnp.where(row_of > k, below, jnp.where(row_of == k, row, work))
    coefficients = jnp.where(lane_of < bands, pltpu.roll(work, width - bands, 1), 0.0)
    inverse_factor = jnp.where(lane_of < bands, pltpu.roll(work, width - 2 * bands, 1), 0.0)
    projected = lax.dot_general(
        inverse_factor,
        coefficients,
        CONTRACT_LANES,
        precision=HIGHEST,
        preferred_element_type=jnp.float32,
    )
    residual = total[bands : bands + 1] - jnp.sum(coefficients * coefficients, axis=0, keepdims=True)
    square_rows = lax.broadcasted_iota(jnp.int32, (bands, bands), 0)
    for r in range(nb):
        mine = me * nb + r
        projected_out[r : r + 1, :] = jnp.sum(
            jnp.where(square_rows == mine, projected, 0.0), axis=0, keepdims=True
        )
        residual_out[r] = jnp.sum(jnp.where(lane_of[0:1] == mine, residual, 0.0))
    out_copy.wait()


def solution(mesh):
    n_band, n_grid = mesh.shape["band"], mesh.shape["grid"]

    def on_device(trial_bands, potential):
        nb, nz, nx, ny = trial_bands.shape
        rows = nz * nx
        bands = nb * n_band
        share = 8 * -(-rows // (8 * n_band))
        width = 128 * -(-3 * bands // 128)
        cells = rows * n_grid * ny
        sizes = (nb, nz, nx, n_band, n_grid, share, width, cells)
        f32 = jnp.float32

        def field(halo):
            return pltpu.VMEM((nb, rows + 2 * halo * nx, ny), f32)

        filtered, projected, residual = pl.pallas_call(
            functools.partial(kernel, sizes),
            out_shape=(
                jax.ShapeDtypeStruct((nb, rows, ny), f32),
                jax.ShapeDtypeStruct((nb, bands), f32),
                jax.ShapeDtypeStruct((nb,), f32),
            ),
            in_specs=[pl.BlockSpec(memory_space=pl.ANY)] * 2,
            out_specs=(
                pl.BlockSpec(memory_space=pl.ANY),
                pl.BlockSpec(memory_space=pltpu.VMEM),
                pl.BlockSpec(memory_space=pltpu.SMEM),
            ),
            scratch_shapes=[
                field(4),
                pltpu.VMEM((rows + 4 * nx, ny), f32),
                field(2),
                field(4),
                field(2),
                field(2),
                pltpu.VMEM((nb, share * n_band, ny), f32),
                pltpu.VMEM((nb, share * n_band, ny), f32),
                pltpu.VMEM((n_band, nb, share, ny), f32),
                pltpu.VMEM((n_band, nb, share, ny), f32),
                pltpu.VMEM((n_band, bands + 8, width), f32),
                pltpu.VMEM((n_grid, bands + 8, width), f32),
                pltpu.SemaphoreType.DMA((8,)),
                pltpu.SemaphoreType.DMA((8,)),
            ]
            + [pltpu.SemaphoreType.DMA((n_band,))] * 6
            + [pltpu.SemaphoreType.DMA((n_grid,))] * 2
            + [pltpu.SemaphoreType.DMA((3,))],
            compiler_params=pltpu.CompilerParams(
                collective_id=0, has_side_effects=True, vmem_limit_bytes=48 * 1024 * 1024
            ),
        )(trial_bands.reshape(nb, rows, ny), potential.reshape(rows, ny))
        return filtered.reshape(nb, nz, nx, ny), projected, residual

    return jax.shard_map(
        on_device,
        mesh=mesh,
        in_specs=(P("band", "grid", None, None), P("grid", None, None)),
        out_specs=(P("band", "grid", None, None), P("band", None), P("band")),
        check_vma=False,
    )
```

```python
import functools

import jax
import jax.numpy as jnp
from jax import lax
from jax.experimental import pallas as pl
from jax.experimental.pallas import tpu as pltpu
from jax.sharding import PartitionSpec as P

CENTER = 4.25
HALF_WIDTH = 3.75
LOWEST = -2.0
SIGMA_ONE = HALF_WIDTH / (LOWEST - CENTER)
MESH = pl.DeviceIdType.MESH
VMEM_LIMIT = 64 * 1024 * 1024
HIGHEST = lax.Precision.HIGHEST
CONTRACT_LANES = (((1,), (1,)), ((), ()))


def filter_steps():
    sigma_now = SIGMA_ONE
    steps = [(SIGMA_ONE / HALF_WIDTH, 0.0)]
    for _ in range(3):
        sigma_next = 1.0 / (2.0 / SIGMA_ONE - sigma_now)
        steps.append((2.0 * sigma_next / HALF_WIDTH, sigma_now * sigma_next))
        sigma_now = sigma_next
    return steps


def kernel(
    sizes,
    x_hbm,
    v_hbm,
    f_out,
    total_out,
    x0,
    vp,
    y1,
    y2,
    y3,
    y4,
    image,
    f_share,
    f_all,
    h_all,
    part_a,
    part_b,
    halo_send,
    halo_recv,
    f_send,
    f_recv,
    h_send,
    h_recv,
    a_send,
    a_recv,
    b_send,
    b_recv,
    local_sem,
):
    nb, nz, nx, n_band, n_grid, share, width = sizes
    rows = nz * nx
    bands = nb * n_band
    me = lax.axis_index("band")
    slab = lax.axis_index("grid")
    right = lax.rem(slab + 1, n_grid)
    left = lax.rem(slab + n_grid - 1, n_grid)
    ny = x0.shape[-1]

    own = [
        pltpu.make_async_copy(x_hbm, x0.at[:, pl.ds(4 * nx, rows)], local_sem.at[0]),
        pltpu.make_async_copy(v_hbm, vp.at[pl.ds(2 * nx, rows)], local_sem.at[1]),
    ]
    for copy in own:
        copy.start()

    barrier = pltpu.get_barrier_semaphore()

    def greet_band(d, carry):
        pl.semaphore_signal(
            barrier, inc=1, device_id=(lax.rem(me + d, n_band), slab), device_id_type=MESH
        )
        return carry

    def greet_grid(d, carry):
        pl.semaphore_signal(
            barrier, inc=1, device_id=(me, lax.rem(slab + d, n_grid)), device_id_type=MESH
        )
        return carry

    lax.fori_loop(1, n_grid, greet_grid, 0)
    lax.fori_loop(1, n_band, greet_band, 0)
    pl.semaphore_wait(barrier, n_band + n_grid - 2)

    def halo_copy(index, src, dst, to):
        return pltpu.make_async_remote_copy(
            src_ref=src,
            dst_ref=dst,
            send_sem=halo_send.at[index],
            recv_sem=halo_recv.at[index],
            device_id=(me, to),
            device_id_type=MESH,
        )

    def up(index, band, src, first, dst, depth):
        return halo_copy(
            2 * (nb * index + band),
            src.at[band, pl.ds((first + nz - depth) * nx, depth * nx)],
            dst.at[band, pl.ds(0, depth * nx)],
            right,
        )

    def down(index, band, src, first, dst, depth):
        return halo_copy(
            2 * (nb * index + band) + 1,
            src.at[band, pl.ds(first * nx, depth * nx)],
            dst.at[band, pl.ds((nz + depth) * nx, depth * nx)],
            left,
        )

    def swap(index, band, src, first, dst, depth):
        return [up(index, band, src, first, dst, depth), down(index, band, src, first, dst, depth)]

    swap_x = [swap(0, band, x_hbm, 0, x0, 4) for band in range(nb)]
    swap_2 = [swap(1, band, y2, 4, y2, 4) for band in range(nb)]
    swap_4 = [swap(2, band, y4, 2, y4, 2) for band in range(nb)]
    swap_v = [
        halo_copy(6 * nb, v_hbm.at[pl.ds((nz - 2) * nx, 2 * nx)], vp.at[pl.ds(0, 2 * nx)], right),
        halo_copy(6 * nb + 1, v_hbm.at[pl.ds(0, 2 * nx)], vp.at[pl.ds((nz + 2) * nx, 2 * nx)], left),
    ]
    for copy in swap_x[0] + swap_v + [copy for band in range(1, nb) for copy in swap_x[band]]:
        copy.start()

    steps = filter_steps()

    def planes(band, lo, hi, src, src_halo, dsts, scale, center, prev=None, prev_halo=0, weight=0.0):
        def at(ref, halo, plane):
            return ref[band, pl.ds(pl.multiple_of((plane + halo) * nx, nx), nx), :]

        def body(step, carry):
            plane = lo + step
            local = vp[pl.ds(pl.multiple_of((plane + 2) * nx, nx), nx), :]
            local = (local + (3.75 - center)) * scale
            here = at(src, src_halo, plane)
            near = at(src, src_halo, plane - 1) + at(src, src_halo, plane + 1)
            far = at(src, src_halo, plane - 2) + at(src, src_halo, plane + 2)
            near += pltpu.roll(here, 1, 0) + pltpu.roll(here, nx - 1, 0)
            far += pltpu.roll(here, 2, 0) + pltpu.roll(here, nx - 2, 0)
            near += pltpu.roll(here, 1, 1) + pltpu.roll(here, ny - 1, 1)
            far += pltpu.roll(here, 2, 1) + pltpu.roll(here, ny - 2, 1)
            value = local * here - near * (scale * 2.0 / 3.0) + far * (scale / 24.0)
            if prev is not None:
                value = value - weight * at(prev, prev_halo, plane)
            for dst, halo in dsts:
                dst[band, pl.ds(pl.multiple_of((plane + halo) * nx, nx), nx), :] = value
            return carry

        lax.fori_loop(0, hi - lo, body, 0, unroll=hi - lo)

    step_1 = functools.partial(planes, src=x0, src_halo=4, dsts=[(y1, 2)], scale=steps[0][0], center=CENTER)
    step_2 = functools.partial(
        planes, src=y1, src_halo=2, dsts=[(y2, 4)], scale=steps[1][0], center=CENTER,
        prev=x0, prev_halo=4, weight=steps[1][1],
    )
    step_3 = functools.partial(
        planes, src=y2, src_halo=4, dsts=[(y3, 2)], scale=steps[2][0], center=CENTER,
        prev=y1, prev_halo=2, weight=steps[2][1],
    )
    step_4 = functools.partial(
        planes, src=y3, src_halo=2, dsts=[(y4, 2), (f_share, 0)], scale=steps[3][0], center=CENTER,
        prev=y2, prev_halo=4, weight=steps[3][1],
    )
    last = functools.partial(planes, src=y4, src_halo=2, dsts=[(image, 0)], scale=1.0, center=0.0)

    padded = share * n_band
    if padded != rows:
        f_share[:, rows:, :] = jnp.zeros((nb, padded - rows, ny), jnp.float32)
        image[:, rows:, :] = jnp.zeros((nb, padded - rows, ny), jnp.float32)

    def to_band(band, src, dst, send, recv, d):
        partner = lax.rem(me + d, n_band)
        return pltpu.make_async_remote_copy(
            src_ref=src.at[band, pl.ds(pl.multiple_of(partner * share, 8), share)],
            dst_ref=dst.at[me, band],
            send_sem=send.at[band, d],
            recv_sem=recv.at[band, n_band - d],
            device_id=(partner, slab),
            device_id_type=MESH,
        )

    def start_band(band, *args):
        def body(d, carry):
            to_band(band, *args, d).start()
            return carry

        lax.fori_loop(1, n_band, body, 0)

    def wait_band(band, *args):
        def body(d, carry):
            to_band(band, *args, d).wait()
            return carry

        lax.fori_loop(1, n_band, body, 0)

    f_route = (f_share, f_all, f_send, f_recv)
    h_route = (image, h_all, h_send, h_recv)

    for copy in own:
        copy.wait()
    for band in range(nb):
        step_1(band, 2, nz - 2)
    for band in range(nb):
        for copy in swap_x[band] + (swap_v if band == 0 else []):
            copy.wait()
        step_1(band, -2, 2)
        step_1(band, nz - 2, nz + 2)
        step_2(band, 0, 4)
        swap_2[band][1].start()
        step_2(band, nz - 4, nz)
        swap_2[band][0].start()
        step_2(band, 4, nz - 4)
    for band in range(nb):
        step_3(band, 2, nz - 2)
        for copy in swap_2[band]:
            copy.wait()
        step_3(band, -2, 2)
        step_3(band, nz - 2, nz + 2)
        step_4(band, 0, 2)
        swap_4[band][1].start()
        step_4(band, nz - 2, nz)
        swap_4[band][0].start()
        step_4(band, 2, nz - 2)
        start_band(band, *f_route)
    out_copy = pltpu.make_async_copy(f_share.at[:, pl.ds(0, rows)], f_out, local_sem.at[2])
    out_copy.start()
    for band in range(nb):
        last(band, 2, nz - 2)
        for copy in swap_4[band]:
            copy.wait()
        last(band, 0, 2)
        last(band, nz - 2, nz)
        start_band(band, *h_route)

    own_rows = pl.ds(pl.multiple_of(me * share, 8), share)
    f_all[me] = f_share[:, own_rows, :]
    h_all[me] = image[:, own_rows, :]

    def on_lanes(ref):
        whole = ref[...]
        tiles = [
            whole[:, :, 8 * t : 8 * t + 8, :].reshape(bands * 8, ny) for t in range(share // 8)
        ]
        return jnp.concatenate(tiles, axis=1)

    stretched = bands * 8
    same = (
        lax.broadcasted_iota(jnp.int32, (stretched, stretched), 0) % 8
        == lax.broadcasted_iota(jnp.int32, (stretched, stretched), 1) % 8
    )
    column = lax.broadcasted_iota(jnp.int32, (stretched, width), 0) // 8
    lane = lax.broadcasted_iota(jnp.int32, (stretched, width), 1)

    def folded(gram, offset):
        gram = jnp.where(same, gram, 0.0).reshape(bands, 8, stretched).sum(axis=1)
        pick = jnp.where(column + offset == lane, 1.0, 0.0)
        return jnp.dot(gram, pick, precision=HIGHEST, preferred_element_type=jnp.float32)

    for band in range(nb):
        wait_band(band, *f_route)
    filtered = on_lanes(f_all)
    margin = lax.dot_general(
        filtered, filtered, CONTRACT_LANES, precision=HIGHEST, preferred_element_type=jnp.float32
    )
    top = folded(margin, 0)
    for band in range(nb):
        wait_band(band, *h_route)
    images = on_lanes(h_all)
    mixed = lax.dot_general(
        filtered, images, CONTRACT_LANES, precision=HIGHEST, preferred_element_type=jnp.float32
    )
    top = top + folded(mixed, bands)
    whole = h_all[...]
    squares = (whole * whole).sum(axis=2).reshape(bands, ny)
    norm_lane = lax.broadcasted_iota(jnp.int32, (bands, width), 1) - 2 * bands * (bands // 8)
    norm_row = lax.broadcasted_iota(jnp.int32, (bands, width), 0)
    norms = jnp.sum(squares, axis=1, keepdims=True)
    norms = jnp.sum(jnp.where(norm_lane == norm_row, norms, 0.0), axis=0, keepdims=True)
    packed = top[0:8]
    for group in range(1, bands // 8):
        packed = packed + pltpu.roll(top[8 * group : 8 * group + 8], 2 * bands * group, 1)
    part_a[me] = packed + norms

    def sum_over(part, count, here, target, send, recv):
        def copy(d):
            return pltpu.make_async_remote_copy(
                src_ref=part.at[here],
                dst_ref=part.at[here],
                send_sem=send.at[d],
                recv_sem=recv.at[count - d],
                device_id=target(lax.rem(here + d, count)),
                device_id_type=MESH,
            )

        def start(d, carry):
            copy(d).start()
            return carry

        def wait(d, carry):
            copy(d).wait()
            return carry

        lax.fori_loop(1, count, start, 0)
        lax.fori_loop(1, count, wait, 0)
        return jnp.sum(part[...], axis=0)

    part_b[slab] = sum_over(part_a, n_band, me, lambda j: (j, slab), a_send, a_recv)
    total_out[...] = sum_over(part_b, n_grid, slab, lambda j: (me, j), b_send, b_recv)
    out_copy.wait()


def small_kernel(sizes, f_in, total_in, f_out, projected_out, residual_out, out_sem):
    nb, bands, width, cells = sizes
    out_copy = pltpu.make_async_copy(f_in, f_out, out_sem)
    out_copy.start()
    me = lax.axis_index("band")
    total = total_in[...] * (1.0 / cells)
    groups = [total] + [
        pltpu.roll(total, width - 2 * bands * group, 1) for group in range(1, bands // 8 + 1)
    ]
    row_of = lax.broadcasted_iota(jnp.int32, (bands, width), 0)
    lane_of = lax.broadcasted_iota(jnp.int32, (bands, width), 1)
    work = jnp.concatenate(groups[:-1], axis=0)
    unit = jnp.where(lane_of == row_of + 2 * bands, 1.0, 0.0)
    work = jnp.where(lane_of < 2 * bands, work, unit)
    for k in range(bands):
        pivot = work[k : k + 1, k : k + 1]
        inverse = lax.rsqrt(pivot)
        inverse = inverse * (1.5 - 0.5 * pivot * inverse * inverse)
        row = work[k : k + 1, :] * inverse
        factor_column = work[:, k : k + 1] * inverse
        below = work - factor_column * row
        work = jnp.where(row_of > k, below, jnp.where(row_of == k, row, work))
    coefficients = jnp.where(lane_of < bands, pltpu.roll(work, width - bands, 1), 0.0)
    inverse_factor = jnp.where(lane_of < bands, pltpu.roll(work, width - 2 * bands, 1), 0.0)
    projected = lax.dot_general(
        inverse_factor,
        coefficients,
        CONTRACT_LANES,
        precision=HIGHEST,
        preferred_element_type=jnp.float32,
    )
    residual = groups[-1][0:1] - jnp.sum(coefficients * coefficients, axis=0, keepdims=True)
    square_rows = lax.broadcasted_iota(jnp.int32, (bands, bands), 0)
    for r in range(nb):
        mine = me * nb + r
        projected_out[r : r + 1, :] = jnp.sum(
            jnp.where(square_rows == mine, projected, 0.0), axis=0, keepdims=True
        )
        residual_out[r] = jnp.sum(jnp.where(lane_of[0:1] == mine, residual, 0.0))
    out_copy.wait()


def solution(mesh):
    n_band, n_grid = mesh.shape["band"], mesh.shape["grid"]

    def on_device(trial_bands, potential):
        nb, nz, nx, ny = trial_bands.shape
        rows = nz * nx
        bands = nb * n_band
        share = 8 * -(-rows // (8 * n_band))
        width = 128 * -(-(2 * bands * (bands // 8) + bands) // 128)
        cells = rows * n_grid * ny
        f32 = jnp.float32

        def field(halo):
            return pltpu.VMEM((nb, rows + 2 * halo * nx, ny), f32)

        shares, total = pl.pallas_call(
            functools.partial(kernel, (nb, nz, nx, n_band, n_grid, share, width)),
            out_shape=(
                jax.ShapeDtypeStruct((nb, rows, ny), f32),
                jax.ShapeDtypeStruct((8, width), f32),
            ),
            in_specs=[pl.BlockSpec(memory_space=pltpu.HBM)] * 2,
            out_specs=(
                pl.BlockSpec(memory_space=pltpu.HBM),
                pl.BlockSpec(memory_space=pltpu.VMEM),
            ),
            scratch_shapes=[
                field(4),
                pltpu.VMEM((rows + 4 * nx, ny), f32),
                field(2),
                field(4),
                field(2),
                field(2),
                pltpu.VMEM((nb, share * n_band, ny), f32),
                pltpu.VMEM((nb, share * n_band, ny), f32),
                pltpu.VMEM((n_band, nb, share, ny), f32),
                pltpu.VMEM((n_band, nb, share, ny), f32),
                pltpu.VMEM((n_band, 8, width), f32),
                pltpu.VMEM((n_grid, 8, width), f32),
                pltpu.SemaphoreType.DMA((6 * nb + 2,)),
                pltpu.SemaphoreType.DMA((6 * nb + 2,)),
            ]
            + [pltpu.SemaphoreType.DMA((nb, n_band))] * 4
            + [pltpu.SemaphoreType.DMA((n_band,))] * 2
            + [pltpu.SemaphoreType.DMA((n_grid,))] * 2
            + [pltpu.SemaphoreType.DMA((3,))],
            compiler_params=pltpu.CompilerParams(
                collective_id=0, has_side_effects=True, vmem_limit_bytes=VMEM_LIMIT
            ),
        )(trial_bands.reshape(nb, rows, ny), potential.reshape(rows, ny))
        filtered, projected, residual = pl.pallas_call(
            functools.partial(small_kernel, (nb, bands, width, cells)),
            out_shape=(
                jax.ShapeDtypeStruct((nb, rows, ny), f32),
                jax.ShapeDtypeStruct((nb, bands), f32),
                jax.ShapeDtypeStruct((nb,), f32),
            ),
            in_specs=[
                pl.BlockSpec(memory_space=pl.ANY),
                pl.BlockSpec(memory_space=pltpu.VMEM),
            ],
            out_specs=(
                pl.BlockSpec(memory_space=pltpu.HBM),
                pl.BlockSpec(memory_space=pltpu.VMEM),
                pl.BlockSpec(memory_space=pltpu.SMEM),
            ),
            scratch_shapes=[pltpu.SemaphoreType.DMA],
            compiler_params=pltpu.CompilerParams(vmem_limit_bytes=VMEM_LIMIT),
        )(shares, total)
        return filtered.reshape(nb, nz, nx, ny), projected, residual

    return jax.shard_map(
        on_device,
        mesh=mesh,
        in_specs=(P("band", "grid", None, None), P("grid", None, None)),
        out_specs=(P("band", "grid", None, None), P("band", None), P("band")),
        check_vma=False,
    )
```

```python
import functools

import jax
import jax.numpy as jnp
from jax import lax
from jax.experimental import pallas as pl
from jax.experimental.pallas import tpu as pltpu
from jax.sharding import PartitionSpec as P

CENTER = 4.25
HALF_WIDTH = 3.75
LOWEST = -2.0
SIGMA_ONE = HALF_WIDTH / (LOWEST - CENTER)
MESH = pl.DeviceIdType.MESH
VMEM_LIMIT = 64 * 1024 * 1024
HIGHEST = lax.Precision.HIGHEST
CONTRACT_LANES = (((1,), (1,)), ((), ()))


def filter_steps():
    sigma_now = SIGMA_ONE
    steps = [(SIGMA_ONE / HALF_WIDTH, 0.0)]
    for _ in range(3):
        sigma_next = 1.0 / (2.0 / SIGMA_ONE - sigma_now)
        steps.append((2.0 * sigma_next / HALF_WIDTH, sigma_now * sigma_next))
        sigma_now = sigma_next
    return steps


def kernel(
    sizes,
    x_hbm,
    v_hbm,
    f_out,
    projected_out,
    residual_out,
    x0,
    vp,
    y1,
    y2,
    y3,
    y4,
    image,
    f_share,
    f_all,
    h_all,
    part_a,
    part_b,
    halo_send,
    halo_recv,
    f_send,
    f_recv,
    h_send,
    h_recv,
    a_send,
    a_recv,
    b_send,
    b_recv,
    local_sem,
):
    nb, nz, nx, n_band, n_grid, share, width, cells = sizes
    rows = nz * nx
    bands = nb * n_band
    me = lax.axis_index("band")
    slab = lax.axis_index("grid")
    right = lax.rem(slab + 1, n_grid)
    left = lax.rem(slab + n_grid - 1, n_grid)
    ny = x0.shape[-1]

    own = [
        pltpu.make_async_copy(x_hbm, x0.at[:, pl.ds(4 * nx, rows)], local_sem.at[0]),
        pltpu.make_async_copy(v_hbm, vp.at[pl.ds(2 * nx, rows)], local_sem.at[1]),
    ]
    for copy in own:
        copy.start()

    barrier = pltpu.get_barrier_semaphore()

    def greet_band(d, carry):
        pl.semaphore_signal(
            barrier, inc=1, device_id=(lax.rem(me + d, n_band), slab), device_id_type=MESH
        )
        return carry

    def greet_grid(d, carry):
        pl.semaphore_signal(
            barrier, inc=1, device_id=(me, lax.rem(slab + d, n_grid)), device_id_type=MESH
        )
        return carry

    lax.fori_loop(1, n_grid, greet_grid, 0)
    lax.fori_loop(1, n_band, greet_band, 0)
    pl.semaphore_wait(barrier, n_band + n_grid - 2)

    def halo_copy(index, src, dst, to):
        return pltpu.make_async_remote_copy(
            src_ref=src,
            dst_ref=dst,
            send_sem=halo_send.at[index],
            recv_sem=halo_recv.at[index],
            device_id=(me, to),
            device_id_type=MESH,
        )

    def up(index, band, src, first, dst, depth):
        return halo_copy(
            2 * (nb * index + band),
            src.at[band, pl.ds((first + nz - depth) * nx, depth * nx)],
            dst.at[band, pl.ds(0, depth * nx)],
            right,
        )

    def down(index, band, src, first, dst, depth):
        return halo_copy(
            2 * (nb * index + band) + 1,
            src.at[band, pl.ds(first * nx, depth * nx)],
            dst.at[band, pl.ds((nz + depth) * nx, depth * nx)],
            left,
        )

    def swap(index, band, src, first, dst, depth):
        return [up(index, band, src, first, dst, depth), down(index, band, src, first, dst, depth)]

    def swap_x(band):
        return swap(0, band, x_hbm, 0, x0, 4)

    def swap_2(band):
        return swap(1, band, y2, 4, y2, 4)

    def swap_4(band):
        return swap(2, band, y4, 2, y4, 2)

    def each_band(body):
        def step(band, carry):
            body(band)
            return carry

        lax.fori_loop(0, nb, step, 0)

    swap_v = [
        halo_copy(6 * nb, v_hbm.at[pl.ds((nz - 2) * nx, 2 * nx)], vp.at[pl.ds(0, 2 * nx)], right),
        halo_copy(6 * nb + 1, v_hbm.at[pl.ds(0, 2 * nx)], vp.at[pl.ds((nz + 2) * nx, 2 * nx)], left),
    ]

    def start_all(copies):
        for copy in copies:
            copy.start()

    def wait_all(copies):
        for copy in copies:
            copy.wait()

    start_all(swap_v)
    each_band(lambda band: start_all(swap_x(band)))

    steps = filter_steps()

    def planes(band, pieces, src, src_halo, dsts, scale, center, prev=None, prev_halo=0, weight=0.0):
        lo, hi = pieces[0]
        pairs = (hi - lo) // 2
        jump = pieces[-1][0] - hi

        def at(ref, halo, plane):
            return ref[band, pl.ds(pl.multiple_of((plane + halo) * nx, nx), nx), :]

        def body(step, carry):
            first = lo + 2 * step + (step // pairs) * jump
            for plane in (first, first + 1):
                local = vp[pl.ds(pl.multiple_of((plane + 2) * nx, nx), nx), :]
                local = (local + (3.75 - center)) * scale
                here = at(src, src_halo, plane)
                near = at(src, src_halo, plane - 1) + at(src, src_halo, plane + 1)
                far = at(src, src_halo, plane - 2) + at(src, src_halo, plane + 2)
                near += pltpu.roll(here, 1, 0) + pltpu.roll(here, nx - 1, 0)
                far += pltpu.roll(here, 2, 0) + pltpu.roll(here, nx - 2, 0)
                near += pltpu.roll(here, 1, 1) + pltpu.roll(here, ny - 1, 1)
                far += pltpu.roll(here, 2, 1) + pltpu.roll(here, ny - 2, 1)
                value = local * here - near * (scale * 2.0 / 3.0) + far * (scale / 24.0)
                if prev is not None:
                    value = value - weight * at(prev, prev_halo, plane)
                for dst, halo in dsts:
                    dst[band, pl.ds(pl.multiple_of((plane + halo) * nx, nx), nx), :] = value
            return carry

        lax.fori_loop(0, pairs * len(pieces), body, 0)

    step_1 = functools.partial(planes, src=x0, src_halo=4, dsts=[(y1, 2)], scale=steps[0][0], center=CENTER)
    step_2 = functools.partial(
        planes, src=y1, src_halo=2, dsts=[(y2, 4)], scale=steps[1][0], center=CENTER,
        prev=x0, prev_halo=4, weight=steps[1][1],
    )
    step_3 = functools.partial(
        planes, src=y2, src_halo=4, dsts=[(y3, 2)], scale=steps[2][0], center=CENTER,
        prev=y1, prev_halo=2, weight=steps[2][1],
    )
    step_4 = functools.partial(
        planes, src=y3, src_halo=2, dsts=[(y4, 2), (f_share, 0)], scale=steps[3][0], center=CENTER,
        prev=y2, prev_halo=4, weight=steps[3][1],
    )
    last = functools.partial(planes, src=y4, src_halo=2, dsts=[(image, 0)], scale=1.0, center=0.0)

    padded = share * n_band
    if padded != rows:
        f_share[:, rows:, :] = jnp.zeros((nb, padded - rows, ny), jnp.float32)
        image[:, rows:, :] = jnp.zeros((nb, padded - rows, ny), jnp.float32)

    def to_band(band, src, dst, send, recv, d):
        partner = lax.rem(me + d, n_band)
        return pltpu.make_async_remote_copy(
            src_ref=src.at[band, pl.ds(pl.multiple_of(partner * share, 8), share)],
            dst_ref=dst.at[me, band],
            send_sem=send.at[band, d],
            recv_sem=recv.at[band, n_band - d],
            device_id=(partner, slab),
            device_id_type=MESH,
        )

    def start_band(band, *args):
        def body(d, carry):
            to_band(band, *args, d).start()
            return carry

        lax.fori_loop(1, n_band, body, 0)

    def wait_band(band, *args):
        def body(d, carry):
            to_band(band, *args, d).wait()
            return carry

        lax.fori_loop(1, n_band, body, 0)

    f_route = (f_share, f_all, f_send, f_recv)
    h_route = (image, h_all, h_send, h_recv)

    inner = [(2, nz - 2)]
    rim = [(0, 2), (nz - 2, nz)]
    halo_rim = [(-2, 2), (nz - 2, nz + 2)]

    def to_y2(band):
        wait_all(swap_x(band))
        step_1(band, halo_rim)
        step_2(band, [(0, 4), (nz - 4, nz)])
        start_all(swap_2(band))
        if nz > 8:
            step_2(band, [(4, nz - 4)])

    def to_y4(band):
        step_3(band, inner)
        wait_all(swap_2(band))
        step_3(band, halo_rim)
        step_4(band, rim)
        start_all(swap_4(band))
        step_4(band, inner)
        start_band(band, *f_route)

    def to_image(band):
        last(band, inner)
        wait_all(swap_4(band))
        last(band, rim)
        start_band(band, *h_route)

    wait_all(own)
    each_band(lambda band: step_1(band, inner))
    wait_all(swap_v)
    each_band(to_y2)
    each_band(to_y4)
    out_copy = pltpu.make_async_copy(f_share.at[:, pl.ds(0, rows)], f_out, local_sem.at[2])
    out_copy.start()
    each_band(to_image)

    own_rows = pl.ds(pl.multiple_of(me * share, 8), share)
    f_all[me] = f_share[:, own_rows, :]
    h_all[me] = image[:, own_rows, :]

    stretched = bands * 8
    same = (
        lax.broadcasted_iota(jnp.int32, (stretched, stretched), 0) % 8
        == lax.broadcasted_iota(jnp.int32, (stretched, stretched), 1) % 8
    )

    def gram(ref):
        def tile(of, t):
            return of[:, :, pl.ds(pl.multiple_of(8 * t, 8), 8), :].reshape(stretched, ny)

        def body(t, total):
            return total + lax.dot_general(
                tile(f_all, t),
                tile(ref, t),
                CONTRACT_LANES,
                precision=HIGHEST,
                preferred_element_type=jnp.float32,
            )

        return lax.fori_loop(0, share // 8, body, jnp.zeros((stretched, stretched), jnp.float32))

    column = lax.broadcasted_iota(jnp.int32, (stretched, width), 0) // 8
    lane = lax.broadcasted_iota(jnp.int32, (stretched, width), 1)

    def folded(products, offset):
        products = jnp.where(same, products, 0.0).reshape(bands, 8, stretched).sum(axis=1)
        pick = jnp.where(column + offset == lane, 1.0, 0.0)
        return jnp.dot(products, pick, precision=HIGHEST, preferred_element_type=jnp.float32)

    each_band(lambda band: wait_band(band, *f_route))
    top = folded(gram(f_all), 0)
    each_band(lambda band: wait_band(band, *h_route))
    top = top + folded(gram(h_all), bands)
    whole = h_all[...]
    squares = (whole * whole).sum(axis=2).reshape(bands, ny)
    norm_lane = lax.broadcasted_iota(jnp.int32, (bands, width), 1) - 2 * bands * (bands // 8)
    norm_row = lax.broadcasted_iota(jnp.int32, (bands, width), 0)
    norms = jnp.sum(squares, axis=1, keepdims=True)
    norms = jnp.sum(jnp.where(norm_lane == norm_row, norms, 0.0), axis=0, keepdims=True)
    packed = top[0:8]
    for group in range(1, bands // 8):
        packed = packed + pltpu.roll(top[8 * group : 8 * group + 8], 2 * bands * group, 1)
    part_a[me] = packed + norms

    def sum_over(part, count, here, target, send, recv):
        def copy(d):
            return pltpu.make_async_remote_copy(
                src_ref=part.at[here],
                dst_ref=part.at[here],
                send_sem=send.at[d],
                recv_sem=recv.at[count - d],
                device_id=target(lax.rem(here + d, count)),
                device_id_type=MESH,
            )

        def start(d, carry):
            copy(d).start()
            return carry

        def wait(d, carry):
            copy(d).wait()
            return carry

        lax.fori_loop(1, count, start, 0)
        lax.fori_loop(1, count, wait, 0)
        return jnp.sum(part[...], axis=0)

    part_b[slab] = sum_over(part_a, n_band, me, lambda j: (j, slab), a_send, a_recv)
    total = sum_over(part_b, n_grid, slab, lambda j: (me, j), b_send, b_recv) * (1.0 / cells)
    groups = [total] + [
        pltpu.roll(total, width - 2 * bands * group, 1) for group in range(1, bands // 8 + 1)
    ]
    row_of = lax.broadcasted_iota(jnp.int32, (bands, width), 0)
    lane_of = lax.broadcasted_iota(jnp.int32, (bands, width), 1)
    work = jnp.concatenate(groups[:-1], axis=0)
    unit = jnp.where(lane_of == row_of + 2 * bands, 1.0, 0.0)
    work = jnp.where(lane_of < 2 * bands, work, unit)
    columns = [jnp.broadcast_to(work[:, k : k + 1], (bands, ny)) for k in range(bands)]
    lane_tile = lax.broadcasted_iota(jnp.int32, (bands, ny), 0)
    pivots = jnp.ones((bands, ny), jnp.float32)
    for k in range(bands):
        own_column = columns[k]
        pivot = jnp.broadcast_to(own_column[k : k + 1], (bands, ny))
        pivots = jnp.where(lane_tile == k, pivot, pivots)
        multiplier = jnp.where(lane_tile > k, own_column, 0.0) / pivot
        work = work - jnp.concatenate([multiplier] * (width // ny), axis=1) * work[k : k + 1]
        for j in range(k + 1, bands):
            columns[j] = columns[j] - multiplier * own_column[j : j + 1]
    work = work / jnp.sqrt(jnp.concatenate([pivots] * (width // ny), axis=1))
    coefficients = jnp.where(lane_of < bands, pltpu.roll(work, width - bands, 1), 0.0)
    inverse_factor = jnp.where(lane_of < bands, pltpu.roll(work, width - 2 * bands, 1), 0.0)
    projected = lax.dot_general(
        inverse_factor,
        coefficients,
        CONTRACT_LANES,
        precision=HIGHEST,
        preferred_element_type=jnp.float32,
    )
    residual = groups[-1][0:1] - jnp.sum(coefficients * coefficients, axis=0, keepdims=True)
    square_rows = lax.broadcasted_iota(jnp.int32, (bands, bands), 0)
    for r in range(nb):
        mine = me * nb + r
        projected_out[r : r + 1, :] = jnp.sum(
            jnp.where(square_rows == mine, projected, 0.0), axis=0, keepdims=True
        )
        residual_out[r] = jnp.sum(jnp.where(lane_of[0:1] == mine, residual, 0.0))
    out_copy.wait()


def solution(mesh):
    n_band, n_grid = mesh.shape["band"], mesh.shape["grid"]

    def on_device(trial_bands, potential):
        nb, nz, nx, ny = trial_bands.shape
        rows = nz * nx
        bands = nb * n_band
        share = 8 * -(-rows // (8 * n_band))
        width = 128 * -(-(2 * bands * (bands // 8) + bands) // 128)
        cells = rows * n_grid * ny
        f32 = jnp.float32

        def field(halo):
            return pltpu.VMEM((nb, rows + 2 * halo * nx, ny), f32)

        filtered, projected, residual = pl.pallas_call(
            functools.partial(kernel, (nb, nz, nx, n_band, n_grid, share, width, cells)),
            out_shape=(
                jax.ShapeDtypeStruct((nb, rows, ny), f32),
                jax.ShapeDtypeStruct((nb, bands), f32),
                jax.ShapeDtypeStruct((nb,), f32),
            ),
            in_specs=[pl.BlockSpec(memory_space=pltpu.HBM)] * 2,
            out_specs=(
                pl.BlockSpec(memory_space=pltpu.HBM),
                pl.BlockSpec(memory_space=pltpu.VMEM),
                pl.BlockSpec(memory_space=pltpu.SMEM),
            ),
            scratch_shapes=[
                field(4),
                pltpu.VMEM((rows + 4 * nx, ny), f32),
                field(2),
                field(4),
                field(2),
                field(2),
                pltpu.VMEM((nb, share * n_band, ny), f32),
                pltpu.VMEM((nb, share * n_band, ny), f32),
                pltpu.VMEM((n_band, nb, share, ny), f32),
                pltpu.VMEM((n_band, nb, share, ny), f32),
                pltpu.VMEM((n_band, 8, width), f32),
                pltpu.VMEM((n_grid, 8, width), f32),
                pltpu.SemaphoreType.DMA((6 * nb + 2,)),
                pltpu.SemaphoreType.DMA((6 * nb + 2,)),
            ]
            + [pltpu.SemaphoreType.DMA((nb, n_band))] * 4
            + [pltpu.SemaphoreType.DMA((n_band,))] * 2
            + [pltpu.SemaphoreType.DMA((n_grid,))] * 2
            + [pltpu.SemaphoreType.DMA((3,))],
            compiler_params=pltpu.CompilerParams(
                collective_id=0, has_side_effects=True, vmem_limit_bytes=VMEM_LIMIT
            ),
        )(trial_bands.reshape(nb, rows, ny), potential.reshape(rows, ny))
        return filtered.reshape(nb, nz, nx, ny), projected, residual

    return jax.shard_map(
        on_device,
        mesh=mesh,
        in_specs=(P("band", "grid", None, None), P("grid", None, None)),
        out_specs=(P("band", "grid", None, None), P("band", None), P("band")),
        check_vma=False,
    )
```

```python
import functools

import jax
import jax.numpy as jnp
from jax import lax
from jax.experimental import pallas as pl
from jax.experimental.pallas import tpu as pltpu
from jax.sharding import PartitionSpec as P

CENTER = 4.25
HALF_WIDTH = 3.75
LOWEST = -2.0
SIGMA_ONE = HALF_WIDTH / (LOWEST - CENTER)
MESH = pl.DeviceIdType.MESH
VMEM_LIMIT = 64 * 1024 * 1024
HIGHEST = lax.Precision.HIGHEST
CONTRACT_LANES = (((1,), (1,)), ((), ()))


def filter_steps():
    sigma_now = SIGMA_ONE
    steps = [(SIGMA_ONE / HALF_WIDTH, 0.0)]
    for _ in range(3):
        sigma_next = 1.0 / (2.0 / SIGMA_ONE - sigma_now)
        steps.append((2.0 * sigma_next / HALF_WIDTH, sigma_now * sigma_next))
        sigma_now = sigma_next
    return steps


def kernel(
    sizes,
    x_hbm,
    v_hbm,
    f_out,
    projected_out,
    residual_out,
    x0,
    vp,
    y1,
    y2,
    y3,
    y4,
    image,
    f_share,
    f_all,
    h_all,
    part_a,
    part_b,
    halo_send,
    halo_recv,
    f_send,
    f_recv,
    h_send,
    h_recv,
    a_send,
    a_recv,
    b_send,
    b_recv,
    local_sem,
):
    nb, nz, nx, n_band, n_grid, share, width, cells = sizes
    rows = nz * nx
    bands = nb * n_band
    me = lax.axis_index("band")
    slab = lax.axis_index("grid")
    right = lax.rem(slab + 1, n_grid)
    left = lax.rem(slab + n_grid - 1, n_grid)
    ny = x0.shape[-1]

    own = [
        pltpu.make_async_copy(x_hbm, x0.at[:, pl.ds(4 * nx, rows)], local_sem.at[0]),
        pltpu.make_async_copy(v_hbm, vp.at[pl.ds(2 * nx, rows)], local_sem.at[1]),
    ]
    for copy in own:
        copy.start()

    barrier = pltpu.get_barrier_semaphore()

    def greet_band(d, carry):
        pl.semaphore_signal(
            barrier, inc=1, device_id=(lax.rem(me + d, n_band), slab), device_id_type=MESH
        )
        return carry

    def greet_grid(d, carry):
        pl.semaphore_signal(
            barrier, inc=1, device_id=(me, lax.rem(slab + d, n_grid)), device_id_type=MESH
        )
        return carry

    lax.fori_loop(1, n_grid, greet_grid, 0)
    lax.fori_loop(1, n_band, greet_band, 0)
    pl.semaphore_wait(barrier, n_band + n_grid - 2)

    def halo_copy(index, src, dst, to):
        return pltpu.make_async_remote_copy(
            src_ref=src,
            dst_ref=dst,
            send_sem=halo_send.at[index],
            recv_sem=halo_recv.at[index],
            device_id=(me, to),
            device_id_type=MESH,
        )

    def swap(index, src, first, dst, depth):
        up = halo_copy(
            2 * index,
            src.at[:, pl.ds((first + nz - depth) * nx, depth * nx)],
            dst.at[:, pl.ds(0, depth * nx)],
            right,
        )
        down = halo_copy(
            2 * index + 1,
            src.at[:, pl.ds(first * nx, depth * nx)],
            dst.at[:, pl.ds((nz + depth) * nx, depth * nx)],
            left,
        )
        return [up, down]

    swap_x = swap(0, x_hbm, 0, x0, 4)
    swap_2 = swap(1, y2, 4, y2, 4)
    swap_4 = swap(2, y4, 2, y4, 2)
    swap_v = [
        halo_copy(6, v_hbm.at[pl.ds((nz - 2) * nx, 2 * nx)], vp.at[pl.ds(0, 2 * nx)], right),
        halo_copy(7, v_hbm.at[pl.ds(0, 2 * nx)], vp.at[pl.ds((nz + 2) * nx, 2 * nx)], left),
    ]

    def start_all(copies):
        for copy in copies:
            copy.start()

    def wait_all(copies):
        for copy in copies:
            copy.wait()

    start_all(swap_v)
    start_all(swap_x)

    steps = filter_steps()

    def planes(firsts, depth, src, src_halo, dsts, scale, center, prev=None, prev_halo=0, weight=0.0):
        def at(ref, band, halo, plane):
            return ref[band, pl.ds(pl.multiple_of((plane + halo) * nx, nx), nx), :]

        def one(plane):
            local = vp[pl.ds(pl.multiple_of((plane + 2) * nx, nx), nx), :]
            local = (local + (3.75 - center)) * scale
            for band in range(nb):
                here = at(src, band, src_halo, plane)
                near = at(src, band, src_halo, plane - 1) + at(src, band, src_halo, plane + 1)
                far = at(src, band, src_halo, plane - 2) + at(src, band, src_halo, plane + 2)
                near += pltpu.roll(here, 1, 0) + pltpu.roll(here, nx - 1, 0)
                far += pltpu.roll(here, 2, 0) + pltpu.roll(here, nx - 2, 0)
                near += pltpu.roll(here, 1, 1) + pltpu.roll(here, ny - 1, 1)
                far += pltpu.roll(here, 2, 1) + pltpu.roll(here, ny - 2, 1)
                value = local * here - near * (scale * 2.0 / 3.0) + far * (scale / 24.0)
                if prev is not None:
                    value = value - weight * at(prev, band, prev_halo, plane)
                for dst, halo in dsts:
                    dst[band, pl.ds(pl.multiple_of((plane + halo) * nx, nx), nx), :] = value

        def body(step, carry):
            for first in firsts:
                for offset in range(group):
                    one(first + step * group + offset)
            return carry

        group = 3 if depth % 3 == 0 else 2
        lax.fori_loop(0, depth // group, body, 0)

    step_1 = functools.partial(planes, src=x0, src_halo=4, dsts=[(y1, 2)], scale=steps[0][0], center=CENTER)
    step_2 = functools.partial(
        planes, src=y1, src_halo=2, dsts=[(y2, 4)], scale=steps[1][0], center=CENTER,
        prev=x0, prev_halo=4, weight=steps[1][1],
    )
    step_3 = functools.partial(
        planes, src=y2, src_halo=4, dsts=[(y3, 2)], scale=steps[2][0], center=CENTER,
        prev=y1, prev_halo=2, weight=steps[2][1],
    )
    step_4 = functools.partial(
        planes, src=y3, src_halo=2, dsts=[(y4, 2), (f_share, 0)], scale=steps[3][0], center=CENTER,
        prev=y2, prev_halo=4, weight=steps[3][1],
    )
    last = functools.partial(planes, src=y4, src_halo=2, dsts=[(image, 0)], scale=1.0, center=0.0)

    padded = share * n_band
    if padded != rows:
        f_share[:, rows:, :] = jnp.zeros((nb, padded - rows, ny), jnp.float32)
        image[:, rows:, :] = jnp.zeros((nb, padded - rows, ny), jnp.float32)

    half = n_band // 2
    side = me // half

    def far_partner(d):
        return (1 - side) * half + lax.rem(me + d, half)

    def near_partner(d):
        return side * half + lax.rem(me + d, half)

    def to_band(partner, src, dst, send, recv):
        return pltpu.make_async_remote_copy(
            src_ref=src.at[:, pl.ds(pl.multiple_of(partner * share, 8), share)],
            dst_ref=dst.at[me],
            send_sem=send.at[partner],
            recv_sem=recv.at[me],
            device_id=(partner, slab),
            device_id_type=MESH,
        )

    def from_band(partner, src, dst, send, recv):
        return pltpu.make_async_remote_copy(
            src_ref=src.at[:, pl.ds(pl.multiple_of(partner * share, 8), share)],
            dst_ref=dst.at[partner],
            send_sem=send.at[partner],
            recv_sem=recv.at[partner],
            device_id=(partner, slab),
            device_id_type=MESH,
        )

    def start_band(*args):
        def far(d, carry):
            to_band(far_partner(d), *args).start()
            return carry

        def near(d, carry):
            to_band(near_partner(d), *args).start()
            return carry

        lax.fori_loop(0, half, far, 0)
        lax.fori_loop(1, half, near, 0)

    def wait_band(*args):
        def body(d, carry):
            from_band(lax.rem(me + d, n_band), *args).wait()
            return carry

        lax.fori_loop(1, n_band, body, 0)

    f_route = (f_share, f_all, f_send, f_recv)
    h_route = (image, h_all, h_send, h_recv)

    wait_all(own)
    step_1((2,), nz - 4)
    wait_all(swap_v)
    wait_all(swap_x)
    step_1((-2, nz - 2), 4)
    step_2((0, nz - 4), 4)
    start_all(swap_2)
    if nz > 8:
        step_2((4,), nz - 8)
    step_3((2,), nz - 4)
    wait_all(swap_2)
    step_3((-2, nz - 2), 4)
    step_4((0, nz - 2), 2)
    start_all(swap_4)
    step_4((2,), nz - 4)
    start_band(*f_route)
    out_copy = pltpu.make_async_copy(f_share.at[:, pl.ds(0, rows)], f_out, local_sem.at[2])
    out_copy.start()
    last((2,), nz - 4)
    wait_all(swap_4)
    last((0, nz - 2), 2)
    start_band(*h_route)

    own_rows = pl.ds(pl.multiple_of(me * share, 8), share)
    f_all[me] = f_share[:, own_rows, :]
    h_all[me] = image[:, own_rows, :]

    stretched = bands * 8
    same = (
        lax.broadcasted_iota(jnp.int32, (stretched, stretched), 0) % 8
        == lax.broadcasted_iota(jnp.int32, (stretched, stretched), 1) % 8
    )

    def gram(ref):
        def tile(of, t):
            return of[:, :, pl.ds(pl.multiple_of(8 * t, 8), 8), :].reshape(stretched, ny)

        def body(t, total):
            return total + lax.dot_general(
                tile(f_all, t),
                tile(ref, t),
                CONTRACT_LANES,
                precision=HIGHEST,
                preferred_element_type=jnp.float32,
            )

        return lax.fori_loop(0, share // 8, body, zero, unroll=unrolled)

    zero = jnp.zeros((stretched, stretched), jnp.float32)
    unrolled = share // 8 if stretched <= 128 else 1
    column = lax.broadcasted_iota(jnp.int32, (stretched, width), 0) // 8
    lane = lax.broadcasted_iota(jnp.int32, (stretched, width), 1)

    def folded(products, offset):
        products = jnp.where(same, products, 0.0).reshape(bands, 8, stretched).sum(axis=1)
        pick = jnp.where(column + offset == lane, 1.0, 0.0)
        return jnp.dot(products, pick, precision=HIGHEST, preferred_element_type=jnp.float32)

    wait_band(*f_route)
    top = folded(gram(f_all), 0)
    wait_band(*h_route)
    top = top + folded(gram(h_all), bands)
    whole = h_all[...]
    squares = (whole * whole).sum(axis=2).reshape(bands, ny)
    norm_lane = lax.broadcasted_iota(jnp.int32, (bands, width), 1) - 2 * bands * (bands // 8)
    norm_row = lax.broadcasted_iota(jnp.int32, (bands, width), 0)
    norms = jnp.sum(squares, axis=1, keepdims=True)
    norms = jnp.sum(jnp.where(norm_lane == norm_row, norms, 0.0), axis=0, keepdims=True)
    packed = top[0:8]
    for group in range(1, bands // 8):
        packed = packed + pltpu.roll(top[8 * group : 8 * group + 8], 2 * bands * group, 1)
    part_a[me] = packed + norms

    def sum_over(part, count, here, target, send, recv):
        def copy(d):
            return pltpu.make_async_remote_copy(
                src_ref=part.at[here],
                dst_ref=part.at[here],
                send_sem=send.at[d],
                recv_sem=recv.at[count - d],
                device_id=target(lax.rem(here + d, count)),
                device_id_type=MESH,
            )

        def start(d, carry):
            copy(d).start()
            return carry

        def wait(d, carry):
            copy(d).wait()
            return carry

        lax.fori_loop(1, count, start, 0)
        lax.fori_loop(1, count, wait, 0)
        return jnp.sum(part[...], axis=0)

    part_b[slab] = sum_over(part_a, n_band, me, lambda j: (j, slab), a_send, a_recv)
    total = sum_over(part_b, n_grid, slab, lambda j: (me, j), b_send, b_recv) * (1.0 / cells)
    groups = [total] + [
        pltpu.roll(total, width - 2 * bands * group, 1) for group in range(1, bands // 8 + 1)
    ]
    row_of = lax.broadcasted_iota(jnp.int32, (bands, width), 0)
    lane_of = lax.broadcasted_iota(jnp.int32, (bands, width), 1)
    work = jnp.concatenate(groups[:-1], axis=0)
    unit = jnp.where(lane_of == row_of + 2 * bands, 1.0, 0.0)
    work = jnp.where(lane_of < 2 * bands, work, unit)
    columns = [jnp.broadcast_to(work[:, k : k + 1], (bands, ny)) for k in range(bands)]
    lane_tile = lax.broadcasted_iota(jnp.int32, (bands, ny), 0)
    pivots = jnp.ones((bands, ny), jnp.float32)
    for k in range(bands):
        own_column = columns[k]
        pivot = jnp.broadcast_to(own_column[k : k + 1], (bands, ny))
        pivots = jnp.where(lane_tile == k, pivot, pivots)
        multiplier = jnp.where(lane_tile > k, own_column, 0.0) / pivot
        work = work - jnp.concatenate([multiplier] * (width // ny), axis=1) * work[k : k + 1]
        for j in range(k + 1, bands):
            columns[j] = columns[j] - multiplier * own_column[j : j + 1]
    work = work / jnp.sqrt(jnp.concatenate([pivots] * (width // ny), axis=1))
    coefficients = jnp.where(lane_of < bands, pltpu.roll(work, width - bands, 1), 0.0)
    inverse_factor = jnp.where(lane_of < bands, pltpu.roll(work, width - 2 * bands, 1), 0.0)
    projected = lax.dot_general(
        inverse_factor,
        coefficients,
        CONTRACT_LANES,
        precision=HIGHEST,
        preferred_element_type=jnp.float32,
    )
    residual = groups[-1][0:1] - jnp.sum(coefficients * coefficients, axis=0, keepdims=True)
    square_rows = lax.broadcasted_iota(jnp.int32, (bands, bands), 0)
    for r in range(nb):
        mine = me * nb + r
        projected_out[r : r + 1, :] = jnp.sum(
            jnp.where(square_rows == mine, projected, 0.0), axis=0, keepdims=True
        )
        residual_out[r] = jnp.sum(jnp.where(lane_of[0:1] == mine, residual, 0.0))
    out_copy.wait()


def solution(mesh):
    n_band, n_grid = mesh.shape["band"], mesh.shape["grid"]

    def on_device(trial_bands, potential):
        nb, nz, nx, ny = trial_bands.shape
        rows = nz * nx
        bands = nb * n_band
        share = 8 * -(-rows // (8 * n_band))
        width = 128 * -(-(2 * bands * (bands // 8) + bands) // 128)
        cells = rows * n_grid * ny
        f32 = jnp.float32

        def field(halo):
            return pltpu.VMEM((nb, rows + 2 * halo * nx, ny), f32)

        filtered, projected, residual = pl.pallas_call(
            functools.partial(kernel, (nb, nz, nx, n_band, n_grid, share, width, cells)),
            out_shape=(
                jax.ShapeDtypeStruct((nb, rows, ny), f32),
                jax.ShapeDtypeStruct((nb, bands), f32),
                jax.ShapeDtypeStruct((nb,), f32),
            ),
            in_specs=[pl.BlockSpec(memory_space=pltpu.HBM)] * 2,
            out_specs=(
                pl.BlockSpec(memory_space=pltpu.HBM),
                pl.BlockSpec(memory_space=pltpu.VMEM),
                pl.BlockSpec(memory_space=pltpu.SMEM),
            ),
            scratch_shapes=[
                field(4),
                pltpu.VMEM((rows + 4 * nx, ny), f32),
                field(2),
                field(4),
                field(2),
                field(2),
                pltpu.VMEM((nb, share * n_band, ny), f32),
                pltpu.VMEM((nb, share * n_band, ny), f32),
                pltpu.VMEM((n_band, nb, share, ny), f32),
                pltpu.VMEM((n_band, nb, share, ny), f32),
                pltpu.VMEM((n_band, 8, width), f32),
                pltpu.VMEM((n_grid, 8, width), f32),
                pltpu.SemaphoreType.DMA((8,)),
                pltpu.SemaphoreType.DMA((8,)),
            ]
            + [pltpu.SemaphoreType.DMA((n_band,))] * 4
            + [pltpu.SemaphoreType.DMA((n_band,))] * 2
            + [pltpu.SemaphoreType.DMA((n_grid,))] * 2
            + [pltpu.SemaphoreType.DMA((3,))],
            compiler_params=pltpu.CompilerParams(
                collective_id=0, has_side_effects=True, vmem_limit_bytes=VMEM_LIMIT
            ),
        )(trial_bands.reshape(nb, rows, ny), potential.reshape(rows, ny))
        return filtered.reshape(nb, nz, nx, ny), projected, residual

    return jax.shard_map(
        on_device,
        mesh=mesh,
        in_specs=(P("band", "grid", None, None), P("grid", None, None)),
        out_specs=(P("band", "grid", None, None), P("band", None), P("band")),
        check_vma=False,
    )
```

```python
import functools

import jax
import jax.numpy as jnp
from jax import lax
from jax.experimental import pallas as pl
from jax.experimental.pallas import tpu as pltpu
from jax.sharding import PartitionSpec as P

CENTER = 4.25
HALF_WIDTH = 3.75
LOWEST = -2.0
SIGMA_ONE = HALF_WIDTH / (LOWEST - CENTER)
MESH = pl.DeviceIdType.MESH
VMEM_LIMIT = 64 * 1024 * 1024
HIGHEST = lax.Precision.HIGHEST
CONTRACT_LANES = (((1,), (1,)), ((), ()))


def filter_steps():
    sigma_now = SIGMA_ONE
    steps = [(SIGMA_ONE / HALF_WIDTH, 0.0)]
    for _ in range(3):
        sigma_next = 1.0 / (2.0 / SIGMA_ONE - sigma_now)
        steps.append((2.0 * sigma_next / HALF_WIDTH, sigma_now * sigma_next))
        sigma_now = sigma_next
    return steps


def kernel(
    sizes,
    x_hbm,
    v_hbm,
    f_out,
    total_out,
    x0,
    vp,
    y1,
    y2,
    y3,
    y4,
    shares,
    gathered,
    part_a,
    part_b,
    halo_send,
    halo_recv,
    share_send,
    share_recv,
    a_send,
    a_recv,
    b_send,
    b_recv,
    local_sem,
):
    nb, nz, nx, n_band, n_grid, share, width = sizes
    rows = nz * nx
    bands = nb * n_band
    me = lax.axis_index("band")
    slab = lax.axis_index("grid")
    right = lax.rem(slab + 1, n_grid)
    left = lax.rem(slab + n_grid - 1, n_grid)
    ny = x0.shape[-1]

    own = [
        pltpu.make_async_copy(x_hbm, x0.at[:, pl.ds(4 * nx, rows)], local_sem.at[0]),
        pltpu.make_async_copy(v_hbm, vp.at[pl.ds(2 * nx, rows)], local_sem.at[1]),
    ]
    for copy in own:
        copy.start()

    barrier = pltpu.get_barrier_semaphore()

    def greet_band(d, carry):
        pl.semaphore_signal(
            barrier, inc=1, device_id=(lax.rem(me + d, n_band), slab), device_id_type=MESH
        )
        return carry

    def greet_grid(d, carry):
        pl.semaphore_signal(
            barrier, inc=1, device_id=(me, lax.rem(slab + d, n_grid)), device_id_type=MESH
        )
        return carry

    lax.fori_loop(1, n_grid, greet_grid, 0)
    lax.fori_loop(1, n_band, greet_band, 0)
    pl.semaphore_wait(barrier, n_band + n_grid - 2)

    def halo_copy(index, src, dst, to):
        return pltpu.make_async_remote_copy(
            src_ref=src,
            dst_ref=dst,
            send_sem=halo_send.at[index],
            recv_sem=halo_recv.at[index],
            device_id=(me, to),
            device_id_type=MESH,
        )

    def up(index, band, src, first, dst, depth):
        return halo_copy(
            2 * (nb * index + band),
            src.at[band, pl.ds((first + nz - depth) * nx, depth * nx)],
            dst.at[band, pl.ds(0, depth * nx)],
            right,
        )

    def down(index, band, src, first, dst, depth):
        return halo_copy(
            2 * (nb * index + band) + 1,
            src.at[band, pl.ds(first * nx, depth * nx)],
            dst.at[band, pl.ds((nz + depth) * nx, depth * nx)],
            left,
        )

    def swap(index, band, src, first, dst, depth):
        return [up(index, band, src, first, dst, depth), down(index, band, src, first, dst, depth)]

    def swap_x(band):
        return swap(0, band, x_hbm, 0, x0, 4)

    def swap_2(band):
        return swap(1, band, y2, 4, y2, 4)

    def swap_4(band):
        return swap(2, band, y4, 2, y4, 2)

    def each_band(body):
        def step(band, carry):
            body(band)
            return carry

        lax.fori_loop(0, nb, step, 0)

    swap_v = [
        halo_copy(6 * nb, v_hbm.at[pl.ds((nz - 2) * nx, 2 * nx)], vp.at[pl.ds(0, 2 * nx)], right),
        halo_copy(6 * nb + 1, v_hbm.at[pl.ds(0, 2 * nx)], vp.at[pl.ds((nz + 2) * nx, 2 * nx)], left),
    ]

    def start_all(copies):
        for copy in copies:
            copy.start()

    def wait_all(copies):
        for copy in copies:
            copy.wait()

    start_all(swap_v)
    each_band(lambda band: start_all(swap_x(band)))

    steps = filter_steps()

    f_share, image = shares.at[0], shares.at[1]

    def planes(band, pieces, src, src_halo, dsts, scale, center, prev=None, prev_halo=0, weight=0.0):
        lo, hi = pieces[0]
        pairs = (hi - lo) // 2
        jump = pieces[-1][0] - hi

        def at(ref, halo, plane):
            return ref[band, pl.ds(pl.multiple_of((plane + halo) * nx, nx), nx), :]

        def body(step, carry):
            first = lo + 2 * step + (step // pairs) * jump
            for plane in (first, first + 1):
                local = vp[pl.ds(pl.multiple_of((plane + 2) * nx, nx), nx), :]
                local = (local + (3.75 - center)) * scale
                here = at(src, src_halo, plane)
                near = at(src, src_halo, plane - 1) + at(src, src_halo, plane + 1)
                far = at(src, src_halo, plane - 2) + at(src, src_halo, plane + 2)
                near += pltpu.roll(here, 1, 0) + pltpu.roll(here, nx - 1, 0)
                far += pltpu.roll(here, 2, 0) + pltpu.roll(here, nx - 2, 0)
                near += pltpu.roll(here, 1, 1) + pltpu.roll(here, ny - 1, 1)
                far += pltpu.roll(here, 2, 1) + pltpu.roll(here, ny - 2, 1)
                value = local * here - near * (scale * 2.0 / 3.0) + far * (scale / 24.0)
                if prev is not None:
                    value = value - weight * at(prev, prev_halo, plane)
                for dst, halo in dsts:
                    dst[band, pl.ds(pl.multiple_of((plane + halo) * nx, nx), nx), :] = value
            return carry

        lax.fori_loop(0, pairs * len(pieces), body, 0)

    step_1 = functools.partial(planes, src=x0, src_halo=4, dsts=[(y1, 2)], scale=steps[0][0], center=CENTER)
    step_2 = functools.partial(
        planes, src=y1, src_halo=2, dsts=[(y2, 4)], scale=steps[1][0], center=CENTER,
        prev=x0, prev_halo=4, weight=steps[1][1],
    )
    step_3 = functools.partial(
        planes, src=y2, src_halo=4, dsts=[(y3, 2)], scale=steps[2][0], center=CENTER,
        prev=y1, prev_halo=2, weight=steps[2][1],
    )
    step_4 = functools.partial(
        planes, src=y3, src_halo=2, dsts=[(y4, 2), (f_share, 0)], scale=steps[3][0], center=CENTER,
        prev=y2, prev_halo=4, weight=steps[3][1],
    )
    last = functools.partial(planes, src=y4, src_halo=2, dsts=[(image, 0)], scale=1.0, center=0.0)

    padded = share * n_band
    if padded != rows:
        shares[:, :, rows:, :] = jnp.zeros((2, nb, padded - rows, ny), jnp.float32)

    def to_band(kind, band, d):
        partner = lax.rem(me + d, n_band)
        return pltpu.make_async_remote_copy(
            src_ref=shares.at[kind, band, pl.ds(pl.multiple_of(partner * share, 8), share)],
            dst_ref=gathered.at[kind, me, band],
            send_sem=share_send.at[kind, band, d],
            recv_sem=share_recv.at[kind, band, n_band - d],
            device_id=(partner, slab),
            device_id_type=MESH,
        )

    def start_band(kind, band):
        def body(d, carry):
            to_band(kind, band, d).start()
            return carry

        lax.fori_loop(1, n_band, body, 0)

    def wait_band(kind, band):
        def body(d, carry):
            to_band(kind, band, d).wait()
            return carry

        lax.fori_loop(1, n_band, body, 0)

    inner = [(2, nz - 2)]
    rim = [(0, 2), (nz - 2, nz)]
    halo_rim = [(-2, 2), (nz - 2, nz + 2)]

    def to_y2(band):
        wait_all(swap_x(band))
        step_1(band, halo_rim)
        step_2(band, [(0, 4), (nz - 4, nz)])
        start_all(swap_2(band))
        if nz > 8:
            step_2(band, [(4, nz - 4)])

    def to_y4(band):
        step_3(band, inner)
        wait_all(swap_2(band))
        step_3(band, halo_rim)
        step_4(band, rim)
        start_all(swap_4(band))
        step_4(band, inner)
        start_band(0, band)

    def to_image(band):
        last(band, inner)
        wait_all(swap_4(band))
        last(band, rim)
        start_band(1, band)

    wait_all(own)
    each_band(lambda band: step_1(band, inner))
    wait_all(swap_v)
    each_band(to_y2)
    each_band(to_y4)
    out_copy = pltpu.make_async_copy(f_share.at[:, pl.ds(0, rows)], f_out, local_sem.at[2])
    out_copy.start()
    each_band(to_image)

    own_rows = pl.ds(pl.multiple_of(me * share, 8), share)
    for kind in range(2):
        gathered[kind, me] = shares[kind, :, own_rows, :]

    stretched = bands * 8
    same = (
        lax.broadcasted_iota(jnp.int32, (stretched, stretched), 0) % 8
        == lax.broadcasted_iota(jnp.int32, (stretched, stretched), 1) % 8
    )

    def gram(kind):
        def tile(of, t):
            part = gathered[of, :, :, pl.ds(pl.multiple_of(8 * t, 8), 8), :]
            return part.reshape(stretched, ny)

        def body(t, total):
            return total + lax.dot_general(
                tile(0, t),
                tile(kind, t),
                CONTRACT_LANES,
                precision=HIGHEST,
                preferred_element_type=jnp.float32,
            )

        return lax.fori_loop(0, share // 8, body, jnp.zeros((stretched, stretched), jnp.float32))

    column = lax.broadcasted_iota(jnp.int32, (stretched, width), 0) // 8
    lane = lax.broadcasted_iota(jnp.int32, (stretched, width), 1)

    def folded(products, offset):
        products = jnp.where(same, products, 0.0).reshape(bands, 8, stretched).sum(axis=1)
        pick = jnp.where(column + offset == lane, 1.0, 0.0)
        return jnp.dot(products, pick, precision=HIGHEST, preferred_element_type=jnp.float32)

    def one_kind(kind, top):
        each_band(lambda band: wait_band(kind, band))
        return top + folded(gram(kind), kind * bands)

    top = lax.fori_loop(0, 2, one_kind, jnp.zeros((bands, width), jnp.float32))
    whole = gathered[1]
    squares = (whole * whole).sum(axis=2).reshape(bands, ny)
    norm_lane = lax.broadcasted_iota(jnp.int32, (bands, width), 1) - 2 * bands * (bands // 8)
    norm_row = lax.broadcasted_iota(jnp.int32, (bands, width), 0)
    norms = jnp.sum(squares, axis=1, keepdims=True)
    norms = jnp.sum(jnp.where(norm_lane == norm_row, norms, 0.0), axis=0, keepdims=True)
    packed = top[0:8]
    for group in range(1, bands // 8):
        packed = packed + pltpu.roll(top[8 * group : 8 * group + 8], 2 * bands * group, 1)
    part_a[me] = packed + norms

    def sum_over(part, count, here, target, send, recv):
        def copy(d):
            return pltpu.make_async_remote_copy(
                src_ref=part.at[here],
                dst_ref=part.at[here],
                send_sem=send.at[d],
                recv_sem=recv.at[count - d],
                device_id=target(lax.rem(here + d, count)),
                device_id_type=MESH,
            )

        def start(d, carry):
            copy(d).start()
            return carry

        def wait(d, carry):
            copy(d).wait()
            return carry

        lax.fori_loop(1, count, start, 0)
        lax.fori_loop(1, count, wait, 0)
        return jnp.sum(part[...], axis=0)

    part_b[slab] = sum_over(part_a, n_band, me, lambda j: (j, slab), a_send, a_recv)
    total_out[...] = sum_over(part_b, n_grid, slab, lambda j: (me, j), b_send, b_recv)
    out_copy.wait()


def small_kernel(sizes, f_in, total_in, f_out, projected_out, residual_out, out_sem):
    nb, bands, width, ny, cells = sizes
    out_copy = pltpu.make_async_copy(f_in, f_out, out_sem)
    out_copy.start()
    me = lax.axis_index("band")
    total = total_in[...] * (1.0 / cells)
    groups = [total] + [
        pltpu.roll(total, width - 2 * bands * group, 1) for group in range(1, bands // 8 + 1)
    ]
    row_of = lax.broadcasted_iota(jnp.int32, (bands, width), 0)
    lane_of = lax.broadcasted_iota(jnp.int32, (bands, width), 1)
    work = jnp.concatenate(groups[:-1], axis=0)
    unit = jnp.where(lane_of == row_of + 2 * bands, 1.0, 0.0)
    work = jnp.where(lane_of < 2 * bands, work, unit)
    columns = [jnp.broadcast_to(work[:, k : k + 1], (bands, ny)) for k in range(bands)]
    lane_tile = lax.broadcasted_iota(jnp.int32, (bands, ny), 0)
    pivots = jnp.ones((bands, ny), jnp.float32)
    for k in range(bands):
        own_column = columns[k]
        pivot = jnp.broadcast_to(own_column[k : k + 1], (bands, ny))
        pivots = jnp.where(lane_tile == k, pivot, pivots)
        multiplier = jnp.where(lane_tile > k, own_column, 0.0) / pivot
        work = work - jnp.concatenate([multiplier] * (width // ny), axis=1) * work[k : k + 1]
        for j in range(k + 1, bands):
            columns[j] = columns[j] - multiplier * own_column[j : j + 1]
    work = work / jnp.sqrt(jnp.concatenate([pivots] * (width // ny), axis=1))
    coefficients = jnp.where(lane_of < bands, pltpu.roll(work, width - bands, 1), 0.0)
    inverse_factor = jnp.where(lane_of < bands, pltpu.roll(work, width - 2 * bands, 1), 0.0)
    projected = lax.dot_general(
        inverse_factor,
        coefficients,
        CONTRACT_LANES,
        precision=HIGHEST,
        preferred_element_type=jnp.float32,
    )
    residual = groups[-1][0:1] - jnp.sum(coefficients * coefficients, axis=0, keepdims=True)
    square_rows = lax.broadcasted_iota(jnp.int32, (bands, bands), 0)
    for r in range(nb):
        mine = me * nb + r
        projected_out[r : r + 1, :] = jnp.sum(
            jnp.where(square_rows == mine, projected, 0.0), axis=0, keepdims=True
        )
        residual_out[r] = jnp.sum(jnp.where(lane_of[0:1] == mine, residual, 0.0))
    out_copy.wait()


def solution(mesh):
    n_band, n_grid = mesh.shape["band"], mesh.shape["grid"]

    def on_device(trial_bands, potential):
        nb, nz, nx, ny = trial_bands.shape
        rows = nz * nx
        bands = nb * n_band
        share = 8 * -(-rows // (8 * n_band))
        width = 128 * -(-(2 * bands * (bands // 8) + bands) // 128)
        cells = rows * n_grid * ny
        f32 = jnp.float32

        def field(halo):
            return pltpu.VMEM((nb, rows + 2 * halo * nx, ny), f32)

        f_held, total = pl.pallas_call(
            functools.partial(kernel, (nb, nz, nx, n_band, n_grid, share, width)),
            out_shape=(
                jax.ShapeDtypeStruct((nb, rows, ny), f32),
                jax.ShapeDtypeStruct((8, width), f32),
            ),
            in_specs=[pl.BlockSpec(memory_space=pltpu.HBM)] * 2,
            out_specs=(
                pl.BlockSpec(memory_space=pltpu.HBM),
                pl.BlockSpec(memory_space=pltpu.VMEM),
            ),
            scratch_shapes=[
                field(4),
                pltpu.VMEM((rows + 4 * nx, ny), f32),
                field(2),
                field(4),
                field(2),
                field(2),
                pltpu.VMEM((2, nb, share * n_band, ny), f32),
                pltpu.VMEM((2, n_band, nb, share, ny), f32),
                pltpu.VMEM((n_band, 8, width), f32),
                pltpu.VMEM((n_grid, 8, width), f32),
                pltpu.SemaphoreType.DMA((6 * nb + 2,)),
                pltpu.SemaphoreType.DMA((6 * nb + 2,)),
            ]
            + [pltpu.SemaphoreType.DMA((2, nb, n_band))] * 2
            + [pltpu.SemaphoreType.DMA((n_band,))] * 2
            + [pltpu.SemaphoreType.DMA((n_grid,))] * 2
            + [pltpu.SemaphoreType.DMA((3,))],
            compiler_params=pltpu.CompilerParams(
                collective_id=0, has_side_effects=True, vmem_limit_bytes=VMEM_LIMIT
            ),
        )(trial_bands.reshape(nb, rows, ny), potential.reshape(rows, ny))
        filtered, projected, residual = pl.pallas_call(
            functools.partial(small_kernel, (nb, bands, width, ny, cells)),
            out_shape=(
                jax.ShapeDtypeStruct((nb, rows, ny), f32),
                jax.ShapeDtypeStruct((nb, bands), f32),
                jax.ShapeDtypeStruct((nb,), f32),
            ),
            in_specs=[
                pl.BlockSpec(memory_space=pltpu.HBM),
                pl.BlockSpec(memory_space=pltpu.VMEM),
            ],
            out_specs=(
                pl.BlockSpec(memory_space=pltpu.HBM),
                pl.BlockSpec(memory_space=pltpu.VMEM),
                pl.BlockSpec(memory_space=pltpu.SMEM),
            ),
            scratch_shapes=[pltpu.SemaphoreType.DMA],
            compiler_params=pltpu.CompilerParams(vmem_limit_bytes=VMEM_LIMIT),
        )(f_held, total)
        return filtered.reshape(nb, nz, nx, ny), projected, residual

    return jax.shard_map(
        on_device,
        mesh=mesh,
        in_specs=(P("band", "grid", None, None), P("grid", None, None)),
        out_specs=(P("band", "grid", None, None), P("band", None), P("band")),
        check_vma=False,
    )
```

```python
import functools

import jax
import jax.numpy as jnp
from jax import lax
from jax.experimental import pallas as pl
from jax.experimental.pallas import tpu as pltpu
from jax.sharding import PartitionSpec as P

CENTER = 4.25
HALF_WIDTH = 3.75
LOWEST = -2.0
SIGMA_ONE = HALF_WIDTH / (LOWEST - CENTER)
MESH = pl.DeviceIdType.MESH
VMEM_LIMIT = 64 * 1024 * 1024
HIGHEST = lax.Precision.HIGHEST
CONTRACT_LANES = (((1,), (1,)), ((), ()))


def filter_steps():
    sigma_now = SIGMA_ONE
    steps = [(SIGMA_ONE / HALF_WIDTH, 0.0)]
    for _ in range(3):
        sigma_next = 1.0 / (2.0 / SIGMA_ONE - sigma_now)
        steps.append((2.0 * sigma_next / HALF_WIDTH, sigma_now * sigma_next))
        sigma_now = sigma_next
    return steps


def kernel(
    sizes,
    x_hbm,
    v_hbm,
    f_out,
    total_out,
    x0,
    vp,
    y1,
    y2,
    y3,
    y4,
    shares,
    gathered,
    part_a,
    part_b,
    halo_send,
    halo_recv,
    share_send,
    share_recv,
    a_send,
    a_recv,
    b_send,
    b_recv,
    local_sem,
):
    nb, nz, nx, n_band, n_grid, share, width = sizes
    rows = nz * nx
    bands = nb * n_band
    me = lax.axis_index("band")
    slab = lax.axis_index("grid")
    right = lax.rem(slab + 1, n_grid)
    left = lax.rem(slab + n_grid - 1, n_grid)
    ny = x0.shape[-1]

    own = [
        pltpu.make_async_copy(x_hbm, x0.at[:, pl.ds(4 * nx, rows)], local_sem.at[0]),
        pltpu.make_async_copy(v_hbm, vp.at[pl.ds(2 * nx, rows)], local_sem.at[1]),
    ]
    for copy in own:
        copy.start()

    barrier = pltpu.get_barrier_semaphore()

    def greet_band(d, carry):
        pl.semaphore_signal(
            barrier, inc=1, device_id=(lax.rem(me + d, n_band), slab), device_id_type=MESH
        )
        return carry

    def greet_grid(d, carry):
        pl.semaphore_signal(
            barrier, inc=1, device_id=(me, lax.rem(slab + d, n_grid)), device_id_type=MESH
        )
        return carry

    lax.fori_loop(1, n_grid, greet_grid, 0)
    lax.fori_loop(1, n_band, greet_band, 0)
    pl.semaphore_wait(barrier, n_band + n_grid - 2)

    def halo_copy(index, src, dst, to):
        return pltpu.make_async_remote_copy(
            src_ref=src,
            dst_ref=dst,
            send_sem=halo_send.at[index],
            recv_sem=halo_recv.at[index],
            device_id=(me, to),
            device_id_type=MESH,
        )

    def up(index, band, src, first, dst, depth):
        return halo_copy(
            2 * (nb * index + band),
            src.at[band, pl.ds((first + nz - depth) * nx, depth * nx)],
            dst.at[band, pl.ds(0, depth * nx)],
            right,
        )

    def down(index, band, src, first, dst, depth):
        return halo_copy(
            2 * (nb * index + band) + 1,
            src.at[band, pl.ds(first * nx, depth * nx)],
            dst.at[band, pl.ds((nz + depth) * nx, depth * nx)],
            left,
        )

    def swap(index, band, src, first, dst, depth):
        return [up(index, band, src, first, dst, depth), down(index, band, src, first, dst, depth)]

    def swap_x(band):
        return swap(0, band, x0, 4, x0, 4)

    def swap_2(band):
        return swap(1, band, y2, 4, y2, 4)

    def swap_4(band):
        return swap(2, band, y4, 2, y4, 2)

    def each_band(body):
        def step(band, carry):
            body(band)
            return carry

        lax.fori_loop(0, nb, step, 0)

    swap_v = [
        halo_copy(6 * nb, vp.at[pl.ds(nz * nx, 2 * nx)], vp.at[pl.ds(0, 2 * nx)], right),
        halo_copy(6 * nb + 1, vp.at[pl.ds(2 * nx, 2 * nx)], vp.at[pl.ds((nz + 2) * nx, 2 * nx)], left),
    ]

    def start_all(copies):
        for copy in copies:
            copy.start()

    def wait_all(copies):
        for copy in copies:
            copy.wait()

    wait_all(own)
    start_all(swap_v)
    each_band(lambda band: start_all(swap_x(band)))

    steps = filter_steps()

    f_share, image = shares.at[0], shares.at[1]

    def planes(band, pieces, src, src_halo, dsts, scale, center, prev=None, prev_halo=0, weight=0.0):
        lo, hi = pieces[0]
        pairs = (hi - lo) // 2
        jump = pieces[-1][0] - hi

        def at(ref, halo, plane):
            return ref[band, pl.ds(pl.multiple_of((plane + halo) * nx, nx), nx), :]

        def body(step, carry):
            first = lo + 2 * step + (step // pairs) * jump
            for plane in (first, first + 1):
                local = vp[pl.ds(pl.multiple_of((plane + 2) * nx, nx), nx), :]
                local = (local + (3.75 - center)) * scale
                here = at(src, src_halo, plane)
                near = at(src, src_halo, plane - 1) + at(src, src_halo, plane + 1)
                far = at(src, src_halo, plane - 2) + at(src, src_halo, plane + 2)
                near += pltpu.roll(here, 1, 0) + pltpu.roll(here, nx - 1, 0)
                far += pltpu.roll(here, 2, 0) + pltpu.roll(here, nx - 2, 0)
                near += pltpu.roll(here, 1, 1) + pltpu.roll(here, ny - 1, 1)
                far += pltpu.roll(here, 2, 1) + pltpu.roll(here, ny - 2, 1)
                value = local * here - near * (scale * 2.0 / 3.0) + far * (scale / 24.0)
                if prev is not None:
                    value = value - weight * at(prev, prev_halo, plane)
                for dst, halo in dsts:
                    dst[band, pl.ds(pl.multiple_of((plane + halo) * nx, nx), nx), :] = value
            return carry

        lax.fori_loop(0, pairs * len(pieces), body, 0)

    step_1 = functools.partial(planes, src=x0, src_halo=4, dsts=[(y1, 2)], scale=steps[0][0], center=CENTER)
    step_2 = functools.partial(
        planes, src=y1, src_halo=2, dsts=[(y2, 4)], scale=steps[1][0], center=CENTER,
        prev=x0, prev_halo=4, weight=steps[1][1],
    )
    step_3 = functools.partial(
        planes, src=y2, src_halo=4, dsts=[(y3, 2)], scale=steps[2][0], center=CENTER,
        prev=y1, prev_halo=2, weight=steps[2][1],
    )
    step_4 = functools.partial(
        planes, src=y3, src_halo=2, dsts=[(y4, 2), (f_share, 0)], scale=steps[3][0], center=CENTER,
        prev=y2, prev_halo=4, weight=steps[3][1],
    )
    last = functools.partial(planes, src=y4, src_halo=2, dsts=[(image, 0)], scale=1.0, center=0.0)

    padded = share * n_band
    if padded != rows:
        shares[:, :, rows:, :] = jnp.zeros((2, nb, padded - rows, ny), jnp.float32)

    def to_band(kind, band, d):
        partner = lax.rem(me + d, n_band)
        return pltpu.make_async_remote_copy(
            src_ref=shares.at[kind, band, pl.ds(pl.multiple_of(partner * share, 8), share)],
            dst_ref=gathered.at[kind, me, band],
            send_sem=share_send.at[kind, band, d],
            recv_sem=share_recv.at[kind, band, n_band - d],
            device_id=(partner, slab),
            device_id_type=MESH,
        )

    def start_band(kind, band):
        def body(d, carry):
            to_band(kind, band, d).start()
            return carry

        lax.fori_loop(1, n_band, body, 0)

    def wait_band(kind, band):
        def body(d, carry):
            to_band(kind, band, d).wait()
            return carry

        lax.fori_loop(1, n_band, body, 0)

    inner = [(2, nz - 2)]
    rim = [(0, 2), (nz - 2, nz)]
    halo_rim = [(-2, 2), (nz - 2, nz + 2)]

    def to_y2(band):
        wait_all(swap_x(band))
        step_1(band, halo_rim)
        step_2(band, [(0, 4), (nz - 4, nz)])
        start_all(swap_2(band))
        if nz > 8:
            step_2(band, [(4, nz - 4)])

    def to_y4(band):
        step_3(band, inner)
        wait_all(swap_2(band))
        step_3(band, halo_rim)
        step_4(band, rim)
        start_all(swap_4(band))
        step_4(band, inner)
        start_band(0, band)

    def to_image(band):
        last(band, inner)
        wait_all(swap_4(band))
        last(band, rim)
        start_band(1, band)

    each_band(lambda band: step_1(band, inner))
    wait_all(swap_v)
    each_band(to_y2)
    each_band(to_y4)
    out_copy = pltpu.make_async_copy(f_share.at[:, pl.ds(0, rows)], f_out, local_sem.at[2])
    out_copy.start()
    each_band(to_image)

    own_rows = pl.ds(pl.multiple_of(me * share, 8), share)
    for kind in range(2):
        gathered[kind, me] = shares[kind, :, own_rows, :]

    stretched = bands * 8
    same = (
        lax.broadcasted_iota(jnp.int32, (stretched, stretched), 0) % 8
        == lax.broadcasted_iota(jnp.int32, (stretched, stretched), 1) % 8
    )

    def gram(kind):
        def tile(of, t):
            part = gathered[of, :, :, pl.ds(pl.multiple_of(8 * t, 8), 8), :]
            return part.reshape(stretched, ny)

        def body(t, total):
            return total + lax.dot_general(
                tile(0, t),
                tile(kind, t),
                CONTRACT_LANES,
                precision=HIGHEST,
                preferred_element_type=jnp.float32,
            )

        return lax.fori_loop(0, share // 8, body, jnp.zeros((stretched, stretched), jnp.float32))

    column = lax.broadcasted_iota(jnp.int32, (stretched, width), 0) // 8
    lane = lax.broadcasted_iota(jnp.int32, (stretched, width), 1)

    def folded(products, offset):
        products = jnp.where(same, products, 0.0).reshape(bands, 8, stretched).sum(axis=1)
        pick = jnp.where(column + offset == lane, 1.0, 0.0)
        return jnp.dot(products, pick, precision=HIGHEST, preferred_element_type=jnp.float32)

    def one_kind(kind, top):
        each_band(lambda band: wait_band(kind, band))
        return top + folded(gram(kind), kind * bands)

    top = lax.fori_loop(0, 2, one_kind, jnp.zeros((bands, width), jnp.float32))
    whole = gathered[1]
    squares = (whole * whole).sum(axis=2).reshape(bands, ny)
    norm_lane = lax.broadcasted_iota(jnp.int32, (bands, width), 1) - 2 * bands * (bands // 8)
    norm_row = lax.broadcasted_iota(jnp.int32, (bands, width), 0)
    norms = jnp.sum(squares, axis=1, keepdims=True)
    norms = jnp.sum(jnp.where(norm_lane == norm_row, norms, 0.0), axis=0, keepdims=True)
    packed = top[0:8]
    for group in range(1, bands // 8):
        packed = packed + pltpu.roll(top[8 * group : 8 * group + 8], 2 * bands * group, 1)
    part_a[me] = packed + norms

    def sum_over(part, count, here, target, send, recv):
        def copy(d):
            return pltpu.make_async_remote_copy(
                src_ref=part.at[here],
                dst_ref=part.at[here],
                send_sem=send.at[d],
                recv_sem=recv.at[count - d],
                device_id=target(lax.rem(here + d, count)),
                device_id_type=MESH,
            )

        def start(d, carry):
            copy(d).start()
            return carry

        def wait(d, carry):
            copy(d).wait()
            return carry

        lax.fori_loop(1, count, start, 0)
        lax.fori_loop(1, count, wait, 0)
        return jnp.sum(part[...], axis=0)

    part_b[slab] = sum_over(part_a, n_band, me, lambda j: (j, slab), a_send, a_recv)
    total_out[...] = sum_over(part_b, n_grid, slab, lambda j: (me, j), b_send, b_recv)
    out_copy.wait()


def small_kernel(sizes, f_in, total_in, f_out, projected_out, residual_out, f_held, out_sem):
    nb, bands, width, ny, cells = sizes
    in_copy = pltpu.make_async_copy(f_in, f_held, out_sem.at[0])
    in_copy.start()
    in_copy.wait()
    out_copy = pltpu.make_async_copy(f_held, f_out, out_sem.at[1])
    out_copy.start()
    me = lax.axis_index("band")
    total = total_in[...] * (1.0 / cells)
    groups = [total] + [
        pltpu.roll(total, width - 2 * bands * group, 1) for group in range(1, bands // 8 + 1)
    ]
    row_of = lax.broadcasted_iota(jnp.int32, (bands, width), 0)
    lane_of = lax.broadcasted_iota(jnp.int32, (bands, width), 1)
    work = jnp.concatenate(groups[:-1], axis=0)
    unit = jnp.where(lane_of == row_of + 2 * bands, 1.0, 0.0)
    work = jnp.where(lane_of < 2 * bands, work, unit)
    columns = [jnp.broadcast_to(work[:, k : k + 1], (bands, ny)) for k in range(bands)]
    lane_tile = lax.broadcasted_iota(jnp.int32, (bands, ny), 0)
    pivots = jnp.ones((bands, ny), jnp.float32)
    for k in range(bands):
        own_column = columns[k]
        pivot = jnp.broadcast_to(own_column[k : k + 1], (bands, ny))
        pivots = jnp.where(lane_tile == k, pivot, pivots)
        multiplier = jnp.where(lane_tile > k, own_column, 0.0) / pivot
        work = work - jnp.concatenate([multiplier] * (width // ny), axis=1) * work[k : k + 1]
        for j in range(k + 1, bands):
            columns[j] = columns[j] - multiplier * own_column[j : j + 1]
    work = work / jnp.sqrt(jnp.concatenate([pivots] * (width // ny), axis=1))
    coefficients = jnp.where(lane_of < bands, pltpu.roll(work, width - bands, 1), 0.0)
    inverse_factor = jnp.where(lane_of < bands, pltpu.roll(work, width - 2 * bands, 1), 0.0)
    projected = lax.dot_general(
        inverse_factor,
        coefficients,
        CONTRACT_LANES,
        precision=HIGHEST,
        preferred_element_type=jnp.float32,
    )
    residual = groups[-1][0:1] - jnp.sum(coefficients * coefficients, axis=0, keepdims=True)
    square_rows = lax.broadcasted_iota(jnp.int32, (bands, bands), 0)
    for r in range(nb):
        mine = me * nb + r
        projected_out[r : r + 1, :] = jnp.sum(
            jnp.where(square_rows == mine, projected, 0.0), axis=0, keepdims=True
        )
        residual_out[r] = jnp.sum(jnp.where(lane_of[0:1] == mine, residual, 0.0))
    out_copy.wait()


def solution(mesh):
    n_band, n_grid = mesh.shape["band"], mesh.shape["grid"]

    def on_device(trial_bands, potential):
        nb, nz, nx, ny = trial_bands.shape
        rows = nz * nx
        bands = nb * n_band
        share = 8 * -(-rows // (8 * n_band))
        width = 128 * -(-(2 * bands * (bands // 8) + bands) // 128)
        cells = rows * n_grid * ny
        f32 = jnp.float32

        def field(halo):
            return pltpu.VMEM((nb, rows + 2 * halo * nx, ny), f32)

        f_held, total = pl.pallas_call(
            functools.partial(kernel, (nb, nz, nx, n_band, n_grid, share, width)),
            out_shape=(
                jax.ShapeDtypeStruct((nb, rows, ny), f32),
                jax.ShapeDtypeStruct((8, width), f32),
            ),
            in_specs=[pl.BlockSpec(memory_space=pltpu.HBM)] * 2,
            out_specs=(
                pl.BlockSpec(memory_space=pltpu.HBM),
                pl.BlockSpec(memory_space=pltpu.VMEM),
            ),
            scratch_shapes=[
                field(4),
                pltpu.VMEM((rows + 4 * nx, ny), f32),
                field(2),
                field(4),
                field(2),
                field(2),
                pltpu.VMEM((2, nb, share * n_band, ny), f32),
                pltpu.VMEM((2, n_band, nb, share, ny), f32),
                pltpu.VMEM((n_band, 8, width), f32),
                pltpu.VMEM((n_grid, 8, width), f32),
                pltpu.SemaphoreType.DMA((6 * nb + 2,)),
                pltpu.SemaphoreType.DMA((6 * nb + 2,)),
            ]
            + [pltpu.SemaphoreType.DMA((2, nb, n_band))] * 2
            + [pltpu.SemaphoreType.DMA((n_band,))] * 2
            + [pltpu.SemaphoreType.DMA((n_grid,))] * 2
            + [pltpu.SemaphoreType.DMA((3,))],
            compiler_params=pltpu.CompilerParams(
                collective_id=0, has_side_effects=True, vmem_limit_bytes=VMEM_LIMIT
            ),
        )(trial_bands.reshape(nb, rows, ny), potential.reshape(rows, ny))
        filtered, projected, residual = pl.pallas_call(
            functools.partial(small_kernel, (nb, bands, width, ny, cells)),
            out_shape=(
                jax.ShapeDtypeStruct((nb, rows, ny), f32),
                jax.ShapeDtypeStruct((nb, bands), f32),
                jax.ShapeDtypeStruct((nb,), f32),
            ),
            in_specs=[
                pl.BlockSpec(memory_space=pltpu.HBM),
                pl.BlockSpec(memory_space=pltpu.VMEM),
            ],
            out_specs=(
                pl.BlockSpec(memory_space=pltpu.HBM),
                pl.BlockSpec(memory_space=pltpu.VMEM),
                pl.BlockSpec(memory_space=pltpu.SMEM),
            ),
            scratch_shapes=[pltpu.VMEM((nb, rows, ny), f32), pltpu.SemaphoreType.DMA((2,))],
            compiler_params=pltpu.CompilerParams(vmem_limit_bytes=VMEM_LIMIT),
        )(f_held, total)
        return filtered.reshape(nb, nz, nx, ny), projected, residual

    return jax.shard_map(
        on_device,
        mesh=mesh,
        in_specs=(P("band", "grid", None, None), P("grid", None, None)),
        out_specs=(P("band", "grid", None, None), P("band", None), P("band")),
        check_vma=False,
    )
```

```python
import functools

import jax
import jax.numpy as jnp
from jax import lax
from jax.experimental import pallas as pl
from jax.experimental.pallas import tpu as pltpu
from jax.sharding import PartitionSpec as P

CENTER = 4.25
HALF_WIDTH = 3.75
LOWEST = -2.0
SIGMA_ONE = HALF_WIDTH / (LOWEST - CENTER)
MESH = pl.DeviceIdType.MESH
VMEM_LIMIT = 64 * 1024 * 1024
HIGHEST = lax.Precision.HIGHEST
CONTRACT_LANES = (((1,), (1,)), ((), ()))


def filter_steps():
    sigma_now = SIGMA_ONE
    steps = [(SIGMA_ONE / HALF_WIDTH, 0.0)]
    for _ in range(3):
        sigma_next = 1.0 / (2.0 / SIGMA_ONE - sigma_now)
        steps.append((2.0 * sigma_next / HALF_WIDTH, sigma_now * sigma_next))
        sigma_now = sigma_next
    return steps


def kernel(
    sizes,
    x_hbm,
    v_hbm,
    f_out,
    total_out,
    x0,
    vp,
    y1,
    y2,
    y3,
    y4,
    shares,
    gathered,
    part_a,
    part_b,
    halo_send,
    halo_recv,
    share_send,
    share_recv,
    a_send,
    a_recv,
    b_send,
    b_recv,
    local_sem,
):
    nb, nz, nx, n_band, n_grid, share, width = sizes
    rows = nz * nx
    bands = nb * n_band
    me = lax.axis_index("band")
    slab = lax.axis_index("grid")
    right = lax.rem(slab + 1, n_grid)
    left = lax.rem(slab + n_grid - 1, n_grid)
    ny = x0.shape[-1]

    own = [
        pltpu.make_async_copy(x_hbm, x0.at[:, pl.ds(4 * nx, rows)], local_sem.at[0]),
        pltpu.make_async_copy(v_hbm, vp.at[pl.ds(2 * nx, rows)], local_sem.at[1]),
    ]
    for copy in own:
        copy.start()

    barrier = pltpu.get_barrier_semaphore()

    def greet_band(d, carry):
        pl.semaphore_signal(
            barrier, inc=1, device_id=(lax.rem(me + d, n_band), slab), device_id_type=MESH
        )
        return carry

    def greet_grid(d, carry):
        pl.semaphore_signal(
            barrier, inc=1, device_id=(me, lax.rem(slab + d, n_grid)), device_id_type=MESH
        )
        return carry

    lax.fori_loop(1, n_grid, greet_grid, 0)
    lax.fori_loop(1, n_band, greet_band, 0)
    pl.semaphore_wait(barrier, n_band + n_grid - 2)

    def halo_copy(index, src, dst, to):
        return pltpu.make_async_remote_copy(
            src_ref=src,
            dst_ref=dst,
            send_sem=halo_send.at[index],
            recv_sem=halo_recv.at[index],
            device_id=(me, to),
            device_id_type=MESH,
        )

    def up(index, band, src, first, dst, depth):
        return halo_copy(
            2 * (nb * index + band),
            src.at[band, pl.ds((first + nz - depth) * nx, depth * nx)],
            dst.at[band, pl.ds(0, depth * nx)],
            right,
        )

    def down(index, band, src, first, dst, depth):
        return halo_copy(
            2 * (nb * index + band) + 1,
            src.at[band, pl.ds(first * nx, depth * nx)],
            dst.at[band, pl.ds((nz + depth) * nx, depth * nx)],
            left,
        )

    def swap(index, band, src, first, dst, depth):
        return [up(index, band, src, first, dst, depth), down(index, band, src, first, dst, depth)]

    def swap_x(band):
        return swap(0, band, x0, 4, x0, 4)

    def swap_2(band):
        return swap(1, band, y2, 4, y2, 4)

    def swap_4(band):
        return swap(2, band, y4, 2, y4, 2)

    def each_band(body):
        def step(band, carry):
            body(band)
            return carry

        lax.fori_loop(0, nb, step, 0)

    swap_v = [
        halo_copy(6 * nb, vp.at[pl.ds(nz * nx, 2 * nx)], vp.at[pl.ds(0, 2 * nx)], right),
        halo_copy(6 * nb + 1, vp.at[pl.ds(2 * nx, 2 * nx)], vp.at[pl.ds((nz + 2) * nx, 2 * nx)], left),
    ]

    def start_all(copies):
        for copy in copies:
            copy.start()

    def wait_all(copies):
        for copy in copies:
            copy.wait()

    wait_all(own)
    start_all(swap_v)
    each_band(lambda band: start_all(swap_x(band)))

    steps = filter_steps()

    f_share, image = shares.at[0], shares.at[1]

    def planes(band, pieces, src, src_halo, dsts, scale, center, prev=None, prev_halo=0, weight=0.0):
        lo, hi = pieces[0]
        pairs = (hi - lo) // 2
        jump = pieces[-1][0] - hi

        def at(ref, halo, plane):
            return ref[band, pl.ds(pl.multiple_of((plane + halo) * nx, nx), nx), :]

        def body(step, carry):
            first = lo + 2 * step + (step // pairs) * jump
            for plane in (first, first + 1):
                local = vp[pl.ds(pl.multiple_of((plane + 2) * nx, nx), nx), :]
                local = (local + (3.75 - center)) * scale
                here = at(src, src_halo, plane)
                near = at(src, src_halo, plane - 1) + at(src, src_halo, plane + 1)
                far = at(src, src_halo, plane - 2) + at(src, src_halo, plane + 2)
                near += pltpu.roll(here, 1, 0) + pltpu.roll(here, nx - 1, 0)
                far += pltpu.roll(here, 2, 0) + pltpu.roll(here, nx - 2, 0)
                near += pltpu.roll(here, 1, 1) + pltpu.roll(here, ny - 1, 1)
                far += pltpu.roll(here, 2, 1) + pltpu.roll(here, ny - 2, 1)
                value = local * here - near * (scale * 2.0 / 3.0) + far * (scale / 24.0)
                if prev is not None:
                    value = value - weight * at(prev, prev_halo, plane)
                for dst, halo in dsts:
                    dst[band, pl.ds(pl.multiple_of((plane + halo) * nx, nx), nx), :] = value
            return carry

        lax.fori_loop(0, pairs * len(pieces), body, 0)

    step_1 = functools.partial(planes, src=x0, src_halo=4, dsts=[(y1, 2)], scale=steps[0][0], center=CENTER)
    step_2 = functools.partial(
        planes, src=y1, src_halo=2, dsts=[(y2, 4)], scale=steps[1][0], center=CENTER,
        prev=x0, prev_halo=4, weight=steps[1][1],
    )
    step_3 = functools.partial(
        planes, src=y2, src_halo=4, dsts=[(y3, 2)], scale=steps[2][0], center=CENTER,
        prev=y1, prev_halo=2, weight=steps[2][1],
    )
    step_4 = functools.partial(
        planes, src=y3, src_halo=2, dsts=[(y4, 2), (f_share, 0)], scale=steps[3][0], center=CENTER,
        prev=y2, prev_halo=4, weight=steps[3][1],
    )
    last = functools.partial(planes, src=y4, src_halo=2, dsts=[(image, 0)], scale=1.0, center=0.0)

    padded = share * n_band
    if padded != rows:
        shares[:, :, rows:, :] = jnp.zeros((2, nb, padded - rows, ny), jnp.float32)

    def to_band(kind, band, d):
        partner = lax.rem(me + d, n_band)
        return pltpu.make_async_remote_copy(
            src_ref=shares.at[kind, band, pl.ds(pl.multiple_of(partner * share, 8), share)],
            dst_ref=gathered.at[kind, me, band],
            send_sem=share_send.at[kind, band, d],
            recv_sem=share_recv.at[kind, band, n_band - d],
            device_id=(partner, slab),
            device_id_type=MESH,
        )

    def start_band(kind, band):
        def body(d, carry):
            to_band(kind, band, d).start()
            return carry

        lax.fori_loop(n_band // 2, n_band, body, 0)
        lax.fori_loop(1, n_band // 2, body, 0)

    def wait_band(kind, band):
        def body(d, carry):
            to_band(kind, band, d).wait()
            return carry

        lax.fori_loop(1, n_band, body, 0)

    inner = [(2, nz - 2)]
    rim = [(0, 2), (nz - 2, nz)]
    halo_rim = [(-2, 2), (nz - 2, nz + 2)]

    def to_y2(band):
        wait_all(swap_x(band))
        step_1(band, halo_rim)
        step_2(band, [(0, 4), (nz - 4, nz)])
        start_all(swap_2(band))
        if nz > 8:
            step_2(band, [(4, nz - 4)])

    def to_y4(band):
        step_3(band, inner)
        wait_all(swap_2(band))
        step_3(band, halo_rim)
        step_4(band, rim)
        start_all(swap_4(band))
        step_4(band, inner)
        start_band(0, band)

    def to_image(band):
        last(band, inner)
        wait_all(swap_4(band))
        last(band, rim)
        start_band(1, band)

    each_band(lambda band: step_1(band, inner))
    wait_all(swap_v)
    each_band(to_y2)
    each_band(to_y4)
    out_copy = pltpu.make_async_copy(f_share.at[:, pl.ds(0, rows)], f_out, local_sem.at[2])
    out_copy.start()
    each_band(to_image)

    own_rows = pl.ds(pl.multiple_of(me * share, 8), share)
    for kind in range(2):
        gathered[kind, me] = shares[kind, :, own_rows, :]

    stretched = bands * 8
    same = (
        lax.broadcasted_iota(jnp.int32, (stretched, stretched), 0) % 8
        == lax.broadcasted_iota(jnp.int32, (stretched, stretched), 1) % 8
    )

    def gram(kind):
        def tile(of, t):
            part = gathered[of, :, :, pl.ds(pl.multiple_of(8 * t, 8), 8), :]
            return part.reshape(stretched, ny)

        def body(t, total):
            return total + lax.dot_general(
                tile(0, t),
                tile(kind, t),
                CONTRACT_LANES,
                precision=HIGHEST,
                preferred_element_type=jnp.float32,
            )

        return lax.fori_loop(0, share // 8, body, jnp.zeros((stretched, stretched), jnp.float32))

    column = lax.broadcasted_iota(jnp.int32, (stretched, width), 0) // 8
    lane = lax.broadcasted_iota(jnp.int32, (stretched, width), 1)

    def folded(products, offset):
        products = jnp.where(same, products, 0.0).reshape(bands, 8, stretched).sum(axis=1)
        pick = jnp.where(column + offset == lane, 1.0, 0.0)
        return jnp.dot(products, pick, precision=HIGHEST, preferred_element_type=jnp.float32)

    def one_kind(kind, top):
        each_band(lambda band: wait_band(kind, band))
        return top + folded(gram(kind), kind * bands)

    top = lax.fori_loop(0, 2, one_kind, jnp.zeros((bands, width), jnp.float32))
    whole = gathered[1]
    squares = (whole * whole).sum(axis=2).reshape(bands, ny)
    norm_lane = lax.broadcasted_iota(jnp.int32, (bands, width), 1) - 2 * bands * (bands // 8)
    norm_row = lax.broadcasted_iota(jnp.int32, (bands, width), 0)
    norms = jnp.sum(squares, axis=1, keepdims=True)
    norms = jnp.sum(jnp.where(norm_lane == norm_row, norms, 0.0), axis=0, keepdims=True)
    packed = top[0:8]
    for group in range(1, bands // 8):
        packed = packed + pltpu.roll(top[8 * group : 8 * group + 8], 2 * bands * group, 1)
    part_a[me] = packed + norms

    def sum_over(part, count, here, target, send, recv):
        def copy(d):
            return pltpu.make_async_remote_copy(
                src_ref=part.at[here],
                dst_ref=part.at[here],
                send_sem=send.at[d],
                recv_sem=recv.at[count - d],
                device_id=target(lax.rem(here + d, count)),
                device_id_type=MESH,
            )

        def start(d, carry):
            copy(d).start()
            return carry

        def wait(d, carry):
            copy(d).wait()
            return carry

        lax.fori_loop(1, count, start, 0)
        lax.fori_loop(1, count, wait, 0)
        return jnp.sum(part[...], axis=0)

    part_b[slab] = sum_over(part_a, n_band, me, lambda j: (j, slab), a_send, a_recv)
    total_out[...] = sum_over(part_b, n_grid, slab, lambda j: (me, j), b_send, b_recv)
    out_copy.wait()


def small_kernel(sizes, f_in, total_in, f_out, projected_out, residual_out, f_held, out_sem):
    nb, bands, width, ny, cells = sizes
    in_copy = pltpu.make_async_copy(f_in, f_held, out_sem.at[0])
    in_copy.start()
    in_copy.wait()
    out_copy = pltpu.make_async_copy(f_held, f_out, out_sem.at[1])
    out_copy.start()
    me = lax.axis_index("band")
    total = total_in[...] * (1.0 / cells)
    groups = [total] + [
        pltpu.roll(total, width - 2 * bands * group, 1) for group in range(1, bands // 8 + 1)
    ]
    row_of = lax.broadcasted_iota(jnp.int32, (bands, width), 0)
    lane_of = lax.broadcasted_iota(jnp.int32, (bands, width), 1)
    work = jnp.concatenate(groups[:-1], axis=0)
    unit = jnp.where(lane_of == row_of + 2 * bands, 1.0, 0.0)
    work = jnp.where(lane_of < 2 * bands, work, unit)
    columns = [jnp.broadcast_to(work[:, k : k + 1], (bands, ny)) for k in range(bands)]
    lane_tile = lax.broadcasted_iota(jnp.int32, (bands, ny), 0)
    pivots = jnp.ones((bands, ny), jnp.float32)
    for k in range(bands):
        own_column = columns[k]
        pivot = jnp.broadcast_to(own_column[k : k + 1], (bands, ny))
        pivots = jnp.where(lane_tile == k, pivot, pivots)
        multiplier = jnp.where(lane_tile > k, own_column, 0.0) / pivot
        work = work - jnp.concatenate([multiplier] * (width // ny), axis=1) * work[k : k + 1]
        for j in range(k + 1, bands):
            columns[j] = columns[j] - multiplier * own_column[j : j + 1]
    work = work / jnp.sqrt(jnp.concatenate([pivots] * (width // ny), axis=1))
    coefficients = jnp.where(lane_of < bands, pltpu.roll(work, width - bands, 1), 0.0)
    inverse_factor = jnp.where(lane_of < bands, pltpu.roll(work, width - 2 * bands, 1), 0.0)
    projected = lax.dot_general(
        inverse_factor,
        coefficients,
        CONTRACT_LANES,
        precision=HIGHEST,
        preferred_element_type=jnp.float32,
    )
    residual = groups[-1][0:1] - jnp.sum(coefficients * coefficients, axis=0, keepdims=True)
    square_rows = lax.broadcasted_iota(jnp.int32, (bands, bands), 0)
    for r in range(nb):
        mine = me * nb + r
        projected_out[r : r + 1, :] = jnp.sum(
            jnp.where(square_rows == mine, projected, 0.0), axis=0, keepdims=True
        )
        residual_out[r] = jnp.sum(jnp.where(lane_of[0:1] == mine, residual, 0.0))
    out_copy.wait()


def solution(mesh):
    n_band, n_grid = mesh.shape["band"], mesh.shape["grid"]

    def on_device(trial_bands, potential):
        nb, nz, nx, ny = trial_bands.shape
        rows = nz * nx
        bands = nb * n_band
        share = 8 * -(-rows // (8 * n_band))
        width = 128 * -(-(2 * bands * (bands // 8) + bands) // 128)
        cells = rows * n_grid * ny
        f32 = jnp.float32

        def field(halo):
            return pltpu.VMEM((nb, rows + 2 * halo * nx, ny), f32)

        f_held, total = pl.pallas_call(
            functools.partial(kernel, (nb, nz, nx, n_band, n_grid, share, width)),
            out_shape=(
                jax.ShapeDtypeStruct((nb, rows, ny), f32),
                jax.ShapeDtypeStruct((8, width), f32),
            ),
            in_specs=[pl.BlockSpec(memory_space=pltpu.HBM)] * 2,
            out_specs=(
                pl.BlockSpec(memory_space=pltpu.HBM),
                pl.BlockSpec(memory_space=pltpu.VMEM),
            ),
            scratch_shapes=[
                field(4),
                pltpu.VMEM((rows + 4 * nx, ny), f32),
                field(2),
                field(4),
                field(2),
                field(2),
                pltpu.VMEM((2, nb, share * n_band, ny), f32),
                pltpu.VMEM((2, n_band, nb, share, ny), f32),
                pltpu.VMEM((n_band, 8, width), f32),
                pltpu.VMEM((n_grid, 8, width), f32),
                pltpu.SemaphoreType.DMA((6 * nb + 2,)),
                pltpu.SemaphoreType.DMA((6 * nb + 2,)),
            ]
            + [pltpu.SemaphoreType.DMA((2, nb, n_band))] * 2
            + [pltpu.SemaphoreType.DMA((n_band,))] * 2
            + [pltpu.SemaphoreType.DMA((n_grid,))] * 2
            + [pltpu.SemaphoreType.DMA((3,))],
            compiler_params=pltpu.CompilerParams(
                collective_id=0, has_side_effects=True, vmem_limit_bytes=VMEM_LIMIT
            ),
        )(trial_bands.reshape(nb, rows, ny), potential.reshape(rows, ny))
        filtered, projected, residual = pl.pallas_call(
            functools.partial(small_kernel, (nb, bands, width, ny, cells)),
            out_shape=(
                jax.ShapeDtypeStruct((nb, rows, ny), f32),
                jax.ShapeDtypeStruct((nb, bands), f32),
                jax.ShapeDtypeStruct((nb,), f32),
            ),
            in_specs=[
                pl.BlockSpec(memory_space=pltpu.HBM),
                pl.BlockSpec(memory_space=pltpu.VMEM),
            ],
            out_specs=(
                pl.BlockSpec(memory_space=pltpu.HBM),
                pl.BlockSpec(memory_space=pltpu.VMEM),
                pl.BlockSpec(memory_space=pltpu.SMEM),
            ),
            scratch_shapes=[pltpu.VMEM((nb, rows, ny), f32), pltpu.SemaphoreType.DMA((2,))],
            compiler_params=pltpu.CompilerParams(vmem_limit_bytes=VMEM_LIMIT),
        )(f_held, total)
        return filtered.reshape(nb, nz, nx, ny), projected, residual

    return jax.shard_map(
        on_device,
        mesh=mesh,
        in_specs=(P("band", "grid", None, None), P("grid", None, None)),
        out_specs=(P("band", "grid", None, None), P("band", None), P("band")),
        check_vma=False,
    )
```
